32 devices in a mesh: image: 4 (over y, core), space: 8 (over z, x).
Axes of the slice: x: 2, y: 2, z: 4, core: 2. Of those that a mesh axis runs over, the one named last changes fastest.
Arguments:
- positions: float32 [4, 3, 1024], P('image', None, 'space'), may hold values from -4 to 12
- velocity: float32 [4, 3, 1024], P('image', None, 'space'), may hold values from -3 to 3
- embed: bfloat16 [1024, 128], P('space'), may hold values from -6 to 6
- neighbours: int32 [1024, 32], P('space'), may hold values from 0 to 383
- send_up: int32 [1024], P('space'), may hold values from 0 to 127
- send_down: int32 [1024], P('space'), may hold values from 0 to 127
- climb: int32 [4], P('image'), may hold values from 0 to 1
- reset: int32 [4], P('image'), may hold values from 0 to 1
- filter_in: float32 [2, 16, 128], replicated, may hold values from -1.5 to 1.5
- filter_out: bfloat16 [2, 128, 128], replicated, may hold values from -0.5 to 0.5
- update_weight: bfloat16 [2, 128, 128], replicated, may hold values from -0.5 to 0.5
- readout: float32 [128], replicated, may hold values from -0.5 to 0.5
- spring: float32 [], replicated, may hold values from 2 to 20
- time_step: float32 [], replicated, may hold values from 0.05 to 0.2
- mixing: float32 [], replicated, may hold values from 0.05 to 0.3
Outputs:
- new_positions: float32 [4, 3, 1024], P('image', None, 'space')
- new_velocity: float32 [4, 3, 1024], P('image', None, 'space')
- energies: float32 [4], P('image')
The draws below stay inside these ranges and needn't reach their ends.
All inputs are finite; a program needn't handle non-finite values.
Results may differ from the reference program's by a relative error of at most 0.0095.
Values may be sent and summed in bfloat16 or wider, within the bound.
A program may use at most 64 MiB of HBM per device.

```python
import math
import jax
import jax.numpy as jnp
from jax import lax

CHANNELS = 128
BASIS = 16
NEIGH_COUNT = 32
LAYERS = 2
ATOM_DEV = 128
GHOST_DEV = 128
IMAGES = 4
ATOMS = 1024
GHOST_ALL = 1024
N_SPACE = 8


def draw_positions(key, part):
    key_base, key_head, key_step, key_noise = jax.random.split(key, 4)
    atom_ids = lax.iota(jnp.int32, ATOMS)
    slab = (atom_ids // ATOM_DEV).astype(jnp.float32)
    fraction = slab / (N_SPACE - 1)
    first_axis = (lax.iota(jnp.int32, 3) == 0).astype(jnp.float32)[:, None]
    base = jax.random.uniform(key_base, (3, ATOMS), jnp.float32) + first_axis * slab[None, :]
    heading = 0.25 * jnp.clip(jax.random.normal(key_head, (3, ATOMS), jnp.float32), -3.0, 3.0)
    progress = (lax.iota(jnp.float32, IMAGES) + 0.4 * jax.random.uniform(key_step, (IMAGES,), jnp.float32)) * (0.8 / IMAGES)
    ramp = 0.4 + 3.6 * fraction
    noise = 0.04 * jnp.clip(jax.random.normal(key_noise, (IMAGES, 3, ATOMS), jnp.float32), -3.5, 3.5)
    return base[None] + ramp[None, None, :] * (progress[:, None, None] * heading[None] + noise)


def place_ends(entries, rng, least, high):
    spot = [jax.random.randint(jax.random.fold_in(rng, axis), (), 0, length) for axis, length in enumerate(entries.shape)]
    widest = entries.shape.index(max(entries.shape))
    neighbour = spot[:widest] + [(spot[widest] + 1) % entries.shape[widest]] + spot[widest + 1:]
    return entries.at[tuple(spot)].set(least).at[tuple(neighbour)].set(high)


def shard_levels(key, dims, cuts, least, largest):
    level = 1.0
    for dim, parts in cuts:
        heights = jax.random.uniform(jax.random.fold_in(jax.random.fold_in(key, 6), dim), (parts,), jnp.float32, least / len(cuts), largest / len(cuts))
        level = level * jnp.repeat(jnp.exp(heights), dims[dim] // parts).reshape((-1,) + (1,) * (len(dims) - 1 - dim))
    return level


def centred(key, shape, scale, most, shards=(), held_as=jnp.bfloat16):
    loudness = shard_levels(key, shape, shards, -0.22, 0.18) if shards else 1.0
    drawn = jax.random.normal(key, shape, jnp.float32) * scale * loudness
    return jnp.minimum(jnp.maximum(drawn, -most), most).astype(held_as)


def setup_inputs(seed: int = 0) -> dict:
    key_of = jax.random.split(jax.random.key(seed), 16)
    positions = draw_positions(jax.random.fold_in(key_of[15], 71), 0)
    velocity = centred(key_of[1], (IMAGES, 3, ATOMS), 0.5, 3.0, ((0, 4), (2, 8)), jnp.float32)
    embed = centred(key_of[2], (ATOMS, CHANNELS), 1.0, 6.0, ((0, 8),))
    neighbours = place_ends(jax.random.randint(key_of[3], (ATOMS, NEIGH_COUNT), 0, ATOM_DEV + 2 * GHOST_DEV), jax.random.fold_in(key_of[3], 1), 0, (ATOM_DEV + 2 * GHOST_DEV) - 1).astype(jnp.int32)
    send_up = place_ends(jax.random.randint(key_of[4], (GHOST_ALL,), 0, ATOM_DEV), jax.random.fold_in(key_of[4], 1), 0, ATOM_DEV - 1).astype(jnp.int32)
    send_down = place_ends(jax.random.randint(key_of[5], (GHOST_ALL,), 0, ATOM_DEV), jax.random.fold_in(key_of[5], 1), 0, ATOM_DEV - 1).astype(jnp.int32)
    climb = place_ends(jax.random.randint(key_of[6], (IMAGES,), 0, 2), jax.random.fold_in(key_of[6], 1), 0, 1).astype(jnp.int32)
    reset = place_ends(jax.random.randint(key_of[7], (IMAGES,), 0, 2), jax.random.fold_in(key_of[7], 1), 0, 1).astype(jnp.int32)
    filter_in = centred(key_of[8], (LAYERS, BASIS, CHANNELS), BASIS ** -0.5, 1.5, (), jnp.float32)
    filter_out = centred(key_of[9], (LAYERS, CHANNELS, CHANNELS), CHANNELS ** -0.5, 0.5)
    update_weight = centred(key_of[10], (LAYERS, CHANNELS, CHANNELS), CHANNELS ** -0.5, 0.5)
    readout = centred(key_of[11], (CHANNELS,), CHANNELS ** -0.5, 0.5, (), jnp.float32)
    spring = jnp.clip(jnp.exp(jax.random.uniform(key_of[12], (), jnp.float32, math.log(2.0), math.log(20.0))), 2.0, 20.0)
    time_step = jnp.clip(jax.random.uniform(key_of[13], (), jnp.float32, 0.05, 0.2), 0.05, 0.2)
    mixing = jnp.clip(jax.random.uniform(key_of[14], (), jnp.float32, 0.05, 0.3), 0.05, 0.3)
    return dict(positions=positions, velocity=velocity, embed=embed, neighbours=neighbours, send_up=send_up, send_down=send_down, climb=climb, reset=reset, filter_in=filter_in, filter_out=filter_out, update_weight=update_weight, readout=readout, spring=spring, time_step=time_step, mixing=mixing)


EPSILON = 1e-06
BASIS_WIDTH = 0.6
BASIS_REACH = 6.0
HIGHEST = lax.Precision.HIGHEST

def silu_grad(values):
    sigmoid = jax.nn.sigmoid(values)
    return sigmoid * (1.0 + values * (1.0 - sigmoid))

def radial(sq_dist, basis_count):
    centres = lax.iota(jnp.float32, basis_count) * (BASIS_REACH / (basis_count - 1))
    scaled = (sq_dist[None, :] - centres[:, None]) / BASIS_WIDTH
    radial_vals = jnp.exp(-scaled * scaled)
    radial_slope = radial_vals * (-2.0 / BASIS_WIDTH) * scaled
    return (radial_vals, radial_slope)

def pair_filter(radial_vals, weight_in, weight_out):
    pre_act = lax.dot_general(radial_vals, weight_in, (((0,), (0,)), ((), ())), precision=HIGHEST, preferred_element_type=jnp.float32)
    activated = jax.nn.silu(pre_act).astype(jnp.bfloat16)
    filter_vals = jnp.dot(activated, weight_out, preferred_element_type=jnp.float32)
    return (pre_act, filter_vals)

def gather_message(filter_vals, source_rows, per_atom):
    product = filter_vals * source_rows.astype(jnp.float32)
    return lax.optimization_barrier(jnp.sum(product.reshape(-1, per_atom, product.shape[1]), axis=1))

def filter_back(grad_msg, source_rows, radial_vals, weight_in, weight_out, per_atom):
    pre_act, filter_vals = pair_filter(radial_vals, weight_in, weight_out)
    repeated = jnp.repeat(grad_msg, per_atom, axis=0)
    grad_filter = (repeated * source_rows.astype(jnp.float32)).astype(jnp.bfloat16)
    grad_source = filter_vals * repeated
    grad_act = lax.dot_general(grad_filter, weight_out, (((1,), (1,)), ((), ())), preferred_element_type=jnp.float32)
    grad_pre = grad_act * silu_grad(pre_act)
    grad_radial = lax.dot_general(weight_in, grad_pre, (((1,), (1,)), ((), ())), precision=HIGHEST, preferred_element_type=jnp.float32)
    return (grad_source, grad_radial)

def image_terms(coords, embed, target, offset, filter_in, filter_out, update_weight, readout):
    per_atom = NEIGH_COUNT
    first_axis = (lax.iota(jnp.int32, 3) == 0).astype(jnp.float32)[:, None]
    flat_ids = target.reshape(-1)
    neighbour_pos = coords[:, flat_ids] + offset.reshape(-1)[None, :] * first_axis
    pair_vec = neighbour_pos - jnp.repeat(coords, per_atom, axis=1)
    sq_dist = lax.optimization_barrier(jnp.sum(pair_vec * pair_vec, axis=0))
    radial_vals, radial_slope = radial(sq_dist, BASIS)
    embed_rows = embed[flat_ids]
    pre_one, filter_one = pair_filter(radial_vals, filter_in[0], filter_out[0])
    message_one = gather_message(filter_one, embed_rows, per_atom).astype(jnp.bfloat16)
    update_one = jnp.dot(message_one, update_weight[0], preferred_element_type=jnp.float32)
    hidden = (embed.astype(jnp.float32) + jax.nn.silu(update_one)).astype(jnp.bfloat16)
    hidden_rows = hidden[flat_ids]
    pre_two, filter_two = pair_filter(radial_vals, filter_in[1], filter_out[1])
    message_two = gather_message(filter_two, hidden_rows, per_atom).astype(jnp.bfloat16)
    update_two = jnp.dot(message_two, update_weight[1], preferred_element_type=jnp.float32)
    energy = jnp.sum(jnp.dot(jax.nn.silu(update_two), readout, precision=HIGHEST))
    grad_update_two = (silu_grad(update_two) * readout[None, :]).astype(jnp.bfloat16)
    grad_msg_two = lax.dot_general(grad_update_two, update_weight[1], (((1,), (1,)), ((), ())), preferred_element_type=jnp.float32)
    grad_source_two, grad_radial_two = filter_back(grad_msg_two, hidden_rows, radial_vals, filter_in[1], filter_out[1], per_atom)
    grad_hidden = jnp.zeros(hidden.shape, jnp.float32).at[flat_ids].add(grad_source_two)
    grad_update_one = (grad_hidden * silu_grad(update_one)).astype(jnp.bfloat16)
    grad_msg_one = lax.dot_general(grad_update_one, update_weight[0], (((1,), (1,)), ((), ())), preferred_element_type=jnp.float32)
    grad_source_one, grad_radial_one = filter_back(grad_msg_one, embed_rows, radial_vals, filter_in[0], filter_out[0], per_atom)
    grad_sq = lax.optimization_barrier(jnp.sum((grad_radial_one + grad_radial_two) * radial_slope, axis=0))
    pair_grad = 2.0 * grad_sq[None, :] * pair_vec
    gradient = jnp.zeros(coords.shape, jnp.float32).at[:, flat_ids].add(pair_grad)
    gradient = gradient - lax.optimization_barrier(jnp.sum(pair_grad.reshape(3, -1, per_atom), axis=2))
    return (energy, -gradient)

def image_sum(values):
    return lax.optimization_barrier(jnp.sum(values, axis=(1, 2)))[:, None, None]

def reference(positions, velocity, embed, neighbours, send_up, send_down, climb, reset, filter_in, filter_out, update_weight, readout, spring, time_step, mixing):
    atom_ids = lax.iota(jnp.int32, ATOMS)
    domain = (atom_ids // ATOM_DEV)[:, None]
    lower_dom = (domain + N_SPACE - 1) % N_SPACE
    upper_dom = (domain + 1) % N_SPACE
    low_slot = jnp.clip(neighbours - ATOM_DEV, 0, GHOST_DEV - 1)
    high_slot = jnp.clip(neighbours - ATOM_DEV - GHOST_DEV, 0, GHOST_DEV - 1)
    from_low = lower_dom * ATOM_DEV + send_up[(lower_dom * GHOST_DEV + low_slot).astype(jnp.int32)]
    from_high = upper_dom * ATOM_DEV + send_down[(upper_dom * GHOST_DEV + high_slot).astype(jnp.int32)]
    own_ids = domain * ATOM_DEV + neighbours
    is_local = neighbours < ATOM_DEV
    is_low = (neighbours >= ATOM_DEV) & (neighbours < ATOM_DEV + GHOST_DEV)
    is_high = neighbours >= ATOM_DEV + GHOST_DEV
    target = jnp.where(is_local, own_ids, jnp.where(is_low, from_low, from_high)).astype(jnp.int32)
    offset = jnp.where(is_low & (domain == 0), -1.0, 0.0) + jnp.where(is_high & (domain == N_SPACE - 1), 1.0, 0.0)
    offset = (offset * N_SPACE).astype(jnp.float32)

    def one_image(coords):
        return image_terms(coords, embed, target, offset, filter_in, filter_out, update_weight, readout)
    energies, forces = lax.map(one_image, positions)
    zero_image = jnp.zeros_like(positions[:1])
    previous = jnp.concatenate([zero_image, positions[:-1]], axis=0)
    following = jnp.concatenate([positions[1:], zero_image], axis=0)
    ahead_vec = following - positions
    behind = positions - previous
    ahead_norm = jnp.sqrt(image_sum(ahead_vec * ahead_vec) + EPSILON)
    behind_norm = jnp.sqrt(image_sum(behind * behind) + EPSILON)
    tangent = ahead_vec / ahead_norm + behind / behind_norm
    unit_tangent = tangent / jnp.sqrt(image_sum(tangent * tangent) + EPSILON)
    parallel = image_sum(forces * unit_tangent)
    image_index = lax.iota(jnp.int32, IMAGES)[:, None, None]
    movable = (image_index > 0) & (image_index < IMAGES - 1)
    climbing = climb[:, None, None] > 0
    spring_part = spring * (ahead_norm - behind_norm)
    band_force = jnp.where(climbing, forces - 2.0 * parallel * unit_tangent, forces - parallel * unit_tangent + spring_part * unit_tangent)
    band_force = jnp.where(movable, band_force, 0.0)
    force_norm = jnp.sqrt(jnp.sum(band_force * band_force) + EPSILON)
    speed_norm = jnp.sqrt(jnp.sum(jnp.where(movable, velocity * velocity, 0.0)) + EPSILON)
    mixed = (1.0 - mixing) * velocity + mixing * (speed_norm / force_norm) * band_force
    kept_speed = jnp.where(reset[:, None, None] > 0, 0.0, mixed)
    new_velocity = jnp.where(movable, kept_speed + time_step * band_force, 0.0)
    new_positions = positions + time_step * new_velocity
    return (new_positions, new_velocity, energies)
```

```python
import functools
import jax
import jax.numpy as jnp
from jax import lax
from jax.experimental import pallas as pl
from jax.experimental.pallas import tpu as pltpu
from jax.sharding import PartitionSpec as P

EPSILON = 1e-06
BASIS_WIDTH = 0.6
BASIS_REACH = 6.0
F32 = jnp.float32
BF16 = jnp.bfloat16
MESH = pl.DeviceIdType.MESH


def dot(left, right):
    return jnp.dot(left, right, preferred_element_type=F32)


def dot_nt(left, right):
    return lax.dot_general(left, right, (((1,), (1,)), ((), ())), preferred_element_type=F32)


def dot_tn(left, right):
    return lax.dot_general(left, right, (((0,), (0,)), ((), ())), preferred_element_type=F32)


def gate(values):
    return 0.5 * jnp.tanh(0.5 * values) + 0.5


def split_two(values):
    high = values.astype(BF16)
    low = (values - high.astype(F32)).astype(BF16)
    return high, low


def onehot(mask):
    return jnp.where(mask, 1.0, 0.0).astype(BF16)


def body(
    n_space, n_image,
    pos_ref, vel_ref, emb_ref, nb_ref, up_ref, down_ref, climb_ref, reset_ref,
    fin_ref, fout_ref, uw_ref, read_ref, spring_ref, step_ref, mix_ref,
    newpos_ref, newvel_ref, energy_ref,
    pos8, prev8, next8, coord, coord_src, ext_emb, emb_src, ext_hid, hid_src,
    grad_all, grad_src, grad_in, force_src, force_in,
    sel, sel_t, oh, oht, nb_t, pv_all, slope_all, pre_two, ds_one, ds_two,
    rows_one, rows_two, filt_two, drad, w_in, w_back,
    norm_src, norm_in, sum_src, sum_in, band_src, band_in,
    send, recv, norm_send, norm_recv, sum_send, sum_recv, band_send, band_recv,
):
    domain = lax.axis_index("space")
    image = lax.axis_index("image")
    upper = lax.rem(domain + 1, n_space)
    lower = lax.rem(domain + n_space - 1, n_space)
    following = lax.rem(image + 1, n_image)
    previous = lax.rem(image + n_image - 1, n_image)
    atoms, per_atom = nb_ref.shape
    ext = 3 * atoms
    chunks, pairs = oh.shape[0], oh.shape[1]
    basis = fin_ref.shape[1]
    channels = emb_ref.shape[1]

    barrier = pltpu.get_barrier_semaphore()
    for i in range(1, n_space):
        pl.semaphore_signal(
            barrier, inc=1, device_id={"space": lax.rem(domain + i, n_space)}, device_id_type=MESH
        )
    for i in range(1, n_image):
        pl.semaphore_signal(
            barrier, inc=1, device_id={"image": lax.rem(image + i, n_image)}, device_id_type=MESH
        )

    def remote(src, dst, slot, where):
        return pltpu.make_async_remote_copy(
            src_ref=src, dst_ref=dst, send_sem=send.at[slot], recv_sem=recv.at[slot],
            device_id=where, device_id_type=MESH,
        )

    def spread(src, dst, out_sem, in_sem, axis, me, count):
        copies = []
        for i in range(1, count):
            copies.append(
                pltpu.make_async_remote_copy(
                    src_ref=src, dst_ref=dst.at[me], send_sem=out_sem.at[i], recv_sem=in_sem.at[me],
                    device_id={axis: lax.rem(me + i, count)}, device_id_type=MESH,
                )
            )
        for copy in copies:
            copy.start()
        dst[me] = src[...]

        def finish():
            for i in range(1, count):
                other = lax.rem(me + i, count)
                pltpu.make_async_remote_copy(
                    src_ref=src, dst_ref=dst.at[other], send_sem=out_sem.at[i],
                    recv_sem=in_sem.at[other], device_id={axis: other}, device_id_type=MESH,
                ).wait_recv()
            for copy in copies:
                copy.wait_send()

        return finish

    pos8[...] = jnp.zeros_like(pos8)
    pos8[0:3, :] = pos_ref[0]
    here = pos8[...]
    part_a = here.astype(BF16).astype(F32)
    rest = here - part_a
    part_b = rest.astype(BF16).astype(F32)
    part_c = rest - part_b
    parts = jnp.concatenate([part_a, part_b, part_c, jnp.zeros_like(here)], axis=0).astype(BF16)
    coord[0] = parts
    atom_rows = lax.broadcasted_iota(jnp.int32, (atoms, atoms), 0)
    embed = emb_ref[...]
    ext_emb[0:atoms, :] = embed
    for side, ids in ((0, up_ref), (1, down_ref)):
        picked = jnp.where(atom_rows == ids[...], 1.0, 0.0)
        sel_t[side] = picked.astype(BF16)
        sel[side] = picked.T.astype(BF16)
        coord_src[side] = dot(parts, sel_t[side]).astype(BF16)
        emb_src[side] = dot(sel[side], embed).astype(BF16)

    pl.semaphore_wait(barrier, n_space + n_image - 2)
    to_up, to_down = {"space": upper}, {"space": lower}
    coord_copies = [
        remote(coord_src.at[0], coord.at[1], 0, to_up),
        remote(coord_src.at[1], coord.at[2], 1, to_down),
    ]
    emb_copies = [
        remote(emb_src.at[0], ext_emb.at[pl.ds(atoms, atoms)], 2, to_up),
        remote(emb_src.at[1], ext_emb.at[pl.ds(2 * atoms, atoms)], 3, to_down),
    ]
    image_copies = [
        remote(pos8, prev8, 4, {"image": following}),
        remote(pos8, next8, 5, {"image": previous}),
    ]
    for copy in coord_copies + emb_copies + image_copies:
        copy.start()

    nb = nb_ref[...]
    nb_t[...] = nb.T
    ext_lane = lax.broadcasted_iota(jnp.int32, (atoms, ext), 1)
    ext_row = lax.broadcasted_iota(jnp.int32, (ext, pairs), 0)
    per_chunk = pairs // atoms
    for k in range(per_atom):
        c, r = k // per_chunk, k % per_chunk
        oh[c, r * atoms : (r + 1) * atoms, :] = onehot(nb[:, k : k + 1] == ext_lane)

    def slot_row(c):
        return jnp.concatenate(
            [nb_t[pl.ds(c * per_chunk + r, 1), :] for r in range(per_chunk)], axis=1
        )

    def build(c, carry):
        oht[c] = onehot(slot_row(c) == ext_row)
        return carry

    lax.fori_loop(0, chunks, build, 0)
    for layer in range(2):
        high, low = split_two(fin_ref[layer])
        lanes = slice(layer * channels, (layer + 1) * channels)
        w_in[:, lanes] = jnp.concatenate([high, high, low], axis=0)
        w_back[layer] = jnp.concatenate([high, low], axis=0)

    for copy in coord_copies + emb_copies:
        copy.wait_recv()

    low_shift = jnp.where(domain == 0, -n_space, 0).astype(F32)
    high_shift = jnp.where(domain == n_space - 1, n_space, 0).astype(F32)
    all_coord = jnp.concatenate([coord[0], coord[1], coord[2]], axis=1)
    here_wide = jnp.concatenate([here] * per_chunk, axis=1)
    first_row = lax.broadcasted_iota(jnp.int32, (8, pairs), 0) == 0
    centres = lax.broadcasted_iota(jnp.int32, (basis, pairs), 0).astype(F32) * (
        BASIS_REACH / (basis - 1)
    )
    ext_embed = ext_emb[...]
    fout_one, fout_two = fout_ref[0], fout_ref[1]

    def fold(values):
        total = values[0:atoms]
        for r in range(1, per_chunk):
            total = total + values[r * atoms : (r + 1) * atoms]
        return total

    def repeat(values):
        return jnp.concatenate([values] * per_chunk, axis=0)

    def layer_one(c, total):
        found = dot(all_coord, oht[c])
        slots = slot_row(c)
        shift = jnp.where(
            slots >= 2 * atoms, high_shift, jnp.where(slots >= atoms, low_shift, 0.0)
        )
        there = found[0:8] + found[8:16] + found[16:24]
        vec = there + jnp.where(first_row, shift, 0.0) - here_wide
        pv_all[c] = vec
        sq_dist = jnp.sum(vec * vec, axis=0, keepdims=True)
        scaled = (sq_dist - centres) * (1.0 / BASIS_WIDTH)
        radial = jnp.exp(-scaled * scaled)
        slope_all[c] = radial * (-2.0 / BASIS_WIDTH) * scaled
        high, low = split_two(radial)
        pre = dot_tn(jnp.concatenate([high, low, high], axis=0), w_in[...])
        pre_two[c] = pre[:, channels:]
        pre_one = pre[:, :channels]
        sig = gate(pre_one)
        act = pre_one * sig
        ds_one[c] = (sig + act * (1.0 - sig)).astype(BF16)
        filt = dot(act.astype(BF16), fout_one)
        rows = dot(oh[c], ext_embed)
        rows_one[c] = rows.astype(BF16)
        return total + fold(filt * rows)

    zeros = jnp.zeros((atoms, channels), F32)
    msg_one = lax.fori_loop(0, chunks, layer_one, zeros)
    upd_one = dot(msg_one.astype(BF16), uw_ref[0])
    sig_one = gate(upd_one)
    act_one = upd_one * sig_one
    slope_one = sig_one + act_one * (1.0 - sig_one)
    hidden = (embed.astype(F32) + act_one).astype(BF16)
    ext_hid[0:atoms, :] = hidden
    hid_src[0] = dot(sel[0], hidden).astype(BF16)
    hid_src[1] = dot(sel[1], hidden).astype(BF16)
    hid_copies = [
        remote(hid_src.at[0], ext_hid.at[pl.ds(atoms, atoms)], 6, to_up),
        remote(hid_src.at[1], ext_hid.at[pl.ds(2 * atoms, atoms)], 7, to_down),
    ]
    for copy in hid_copies:
        copy.start()

    for copy in image_copies:
        copy.wait_recv()
    ahead = jnp.where(image == n_image - 1, 0.0, next8[...]) - here
    behind = here - jnp.where(image == 0, 0.0, prev8[...])
    row8 = lax.broadcasted_iota(jnp.int32, (8, atoms), 0)

    def place(values):
        block = jnp.zeros((8, atoms), F32)
        for r, value in enumerate(values):
            block = jnp.where(row8 == r, value, block)
        return block

    def rows_sum(values):
        return jnp.sum(values, axis=0, keepdims=True)

    norm_src[...] = place([rows_sum(ahead * ahead), rows_sum(behind * behind)])
    norm_done = spread(norm_src, norm_in, norm_send, norm_recv, "space", domain, n_space)

    def filter_two(c, carry):
        pre = pre_two[c]
        sig = gate(pre)
        act = pre * sig
        ds_two[c] = (sig + act * (1.0 - sig)).astype(BF16)
        filt_two[c] = dot(act.astype(BF16), fout_two)
        return carry

    lax.fori_loop(0, chunks, filter_two, 0)
    for copy in hid_copies:
        copy.wait_recv()
    ext_hidden = ext_hid[...]

    def layer_two(c, total):
        rows = dot(oh[c], ext_hidden)
        rows_two[c] = rows.astype(BF16)
        return total + fold(filt_two[c] * rows)

    msg_two = lax.fori_loop(0, chunks, layer_two, zeros)
    upd_two = dot(msg_two.astype(BF16), uw_ref[1])
    sig_two = gate(upd_two)
    act_two = upd_two * sig_two
    readout = read_ref[...]
    energy_row = rows_sum(act_two * readout)
    dupd_two = ((sig_two + act_two * (1.0 - sig_two)) * readout).astype(BF16)
    dmsg_two = dot_nt(dupd_two, uw_ref[1])

    grad_all[...] = jnp.zeros_like(grad_all)

    def scatter_two(c, carry):
        source = (filt_two[c] * repeat(dmsg_two)).astype(BF16)
        grad_all[...] += dot(oht[c], source)
        return carry

    lax.fori_loop(0, chunks, scatter_two, 0)
    grad_src[0] = grad_all[atoms : 2 * atoms, :].astype(BF16)
    grad_src[1] = grad_all[2 * atoms : 3 * atoms, :].astype(BF16)
    grad_copies = [
        remote(grad_src.at[0], grad_in.at[0], 8, to_down),
        remote(grad_src.at[1], grad_in.at[1], 9, to_up),
    ]
    for copy in grad_copies:
        copy.start()

    def back(dmsg, rows, weight, slope, layer):
        dfilt = (repeat(dmsg) * rows.astype(F32)).astype(BF16)
        dact = dot_nt(dfilt, weight)
        dpre = (dact * slope.astype(F32)).astype(BF16)
        both = dot_nt(w_back[layer], dpre)
        return both[:basis] + both[basis:]

    def back_two(c, carry):
        drad[c] = back(dmsg_two, rows_two[c], fout_two, ds_two[c], 1)
        return carry

    lax.fori_loop(0, chunks, back_two, 0)
    for copy in grad_copies:
        copy.wait_recv()
    dhidden = grad_all[0:atoms, :] + dot(sel_t[0], grad_in[0]) + dot(sel_t[1], grad_in[1])
    dupd_one = (dhidden * slope_one).astype(BF16)
    dmsg_one = dot_nt(dupd_one, uw_ref[0])

    def back_one(c, carry):
        own, scattered = carry
        dradial = drad[c] + back(dmsg_one, rows_one[c], fout_one, ds_one[c], 0)
        dsq = jnp.sum(dradial * slope_all[c], axis=0, keepdims=True)
        pair = (2.0 * dsq) * pv_all[c]
        for r in range(per_chunk):
            own = own + pair[:, r * atoms : (r + 1) * atoms]
        high = pair.astype(BF16).astype(F32)
        both = jnp.concatenate([high, pair - high], axis=0).astype(BF16)
        return own, scattered + dot(both, oh[c])

    own, scattered = lax.fori_loop(
        0, chunks, back_one, (jnp.zeros((8, atoms), F32), jnp.zeros((16, ext), F32))
    )
    scattered = scattered[0:8] + scattered[8:16]
    force_src[0] = scattered[:, atoms : 2 * atoms]
    force_src[1] = scattered[:, 2 * atoms : 3 * atoms]
    force_copies = [
        remote(force_src.at[0], force_in.at[0], 10, to_down),
        remote(force_src.at[1], force_in.at[1], 11, to_up),
    ]
    for copy in force_copies:
        copy.start()

    norm_done()
    norm_sum = norm_in[0]
    for i in range(1, n_space):
        norm_sum = norm_sum + norm_in[i]
    norms = jnp.sqrt(jnp.sum(norm_sum, axis=1, keepdims=True) + EPSILON)
    ahead_norm, behind_norm = norms[0:1], norms[1:2]
    tangent = ahead / ahead_norm + behind / behind_norm
    tangent_row = rows_sum(tangent * tangent)
    speed = jnp.concatenate([vel_ref[0], jnp.zeros((5, atoms), F32)], axis=0)
    speed_row = rows_sum(speed * speed)
    spring_part = spring_ref[0, 0] * (ahead_norm - behind_norm)
    local_force = own - scattered[:, 0:atoms]
    for copy in force_copies:
        copy.wait_recv()

    def returned(side):
        ghost = force_in[side]
        high = ghost.astype(BF16).astype(F32)
        both = dot(jnp.concatenate([high, ghost - high], axis=0).astype(BF16), sel[side])
        return both[0:8] + both[8:16]

    forces = local_force - returned(0) - returned(1)
    sum_src[...] = place(
        [
            rows_sum(forces * forces), rows_sum(forces * tangent), tangent_row, energy_row,
            speed_row,
        ]
    )
    sum_done = spread(sum_src, sum_in, sum_send, sum_recv, "space", domain, n_space)
    sum_done()
    sums = sum_in[0]
    for i in range(1, n_space):
        sums = sums + sum_in[i]
    sums = jnp.sum(sums, axis=1, keepdims=True)
    force_sq, along, tangent_sq = sums[0:1], sums[1:2], sums[2:3]
    energy_ref[...] = sums[3:4]
    scale = 1.0 / jnp.sqrt(tangent_sq + EPSILON)
    parallel = along * scale
    unit_sq = tangent_sq * scale * scale
    climbing = climb_ref[0] > 0
    take = jnp.where(climbing, 2.0 * parallel, parallel - spring_part)
    movable = jnp.where((image > 0) & (image < n_image - 1), 1.0, 0.0)
    band_sq = jnp.maximum(force_sq - 2.0 * take * parallel + take * take * unit_sq, 0.0)
    band_src[...] = place([band_sq * movable, sums[4:5] * movable])
    band_done = spread(band_src, band_in, band_send, band_recv, "image", image, n_image)
    band_force = (forces - take * (tangent * scale)) * movable
    band_done()
    totals = band_in[0]
    for i in range(1, n_image):
        totals = totals + band_in[i]
    totals = jnp.sqrt(totals + EPSILON)
    force_norm, speed_norm = totals[0:1], totals[1:2]
    mixing = mix_ref[0, 0]
    time_step = step_ref[0, 0]
    mixed = (1.0 - mixing) * speed + mixing * (speed_norm / force_norm) * band_force
    kept = jnp.where(reset_ref[0] > 0, 0.0, mixed)
    new_speed = (kept + time_step * band_force) * movable
    newvel_ref[0] = new_speed[0:3]
    newpos_ref[0] = (here + time_step * new_speed)[0:3]
    for copy in (
        coord_copies + emb_copies + image_copies + hid_copies + grad_copies + force_copies
    ):
        copy.wait_send()


def per_device(
    n_space, n_image,
    positions, velocity, embed, neighbours, send_up, send_down, climb, reset,
    filter_in, filter_out, update_weight, readout, spring, time_step, mixing,
):
    atoms, per_atom = neighbours.shape
    channels = embed.shape[1]
    basis = filter_in.shape[1]
    per_chunk = 2
    chunks, pairs = per_atom // per_chunk, per_chunk * atoms
    ext = 3 * atoms
    vmem = pl.BlockSpec(memory_space=pltpu.VMEM)
    smem = pl.BlockSpec(memory_space=pltpu.SMEM)
    dma = pltpu.SemaphoreType.DMA
    scratch = [
        pltpu.VMEM((8, atoms), F32),
        pltpu.VMEM((8, atoms), F32),
        pltpu.VMEM((8, atoms), F32),
        pltpu.VMEM((3, 32, atoms), BF16),
        pltpu.VMEM((2, 32, atoms), BF16),
        pltpu.VMEM((ext, channels), BF16),
        pltpu.VMEM((2, atoms, channels), BF16),
        pltpu.VMEM((ext, channels), BF16),
        pltpu.VMEM((2, atoms, channels), BF16),
        pltpu.VMEM((ext, channels), F32),
        pltpu.VMEM((2, atoms, channels), BF16),
        pltpu.VMEM((2, atoms, channels), BF16),
        pltpu.VMEM((2, 8, atoms), F32),
        pltpu.VMEM((2, 8, atoms), F32),
        pltpu.VMEM((2, atoms, atoms), BF16),
        pltpu.VMEM((2, atoms, atoms), BF16),
        pltpu.VMEM((chunks, pairs, ext), BF16),
        pltpu.VMEM((chunks, ext, pairs), BF16),
        pltpu.VMEM((per_atom, atoms), jnp.int32),
        pltpu.VMEM((chunks, 8, pairs), F32),
        pltpu.VMEM((chunks, basis, pairs), F32),
        pltpu.VMEM((chunks, pairs, channels), F32),
        pltpu.VMEM((chunks, pairs, channels), BF16),
        pltpu.VMEM((chunks, pairs, channels), BF16),
        pltpu.VMEM((chunks, pairs, channels), BF16),
        pltpu.VMEM((chunks, pairs, channels), BF16),
        pltpu.VMEM((chunks, pairs, channels), F32),
        pltpu.VMEM((chunks, basis, pairs), F32),
        pltpu.VMEM((3 * basis, 2 * channels), BF16),
        pltpu.VMEM((2, 2 * basis, channels), BF16),
        pltpu.VMEM((8, atoms), F32),
        pltpu.VMEM((n_space, 8, atoms), F32),
        pltpu.VMEM((8, atoms), F32),
        pltpu.VMEM((n_space, 8, atoms), F32),
        pltpu.VMEM((8, atoms), F32),
        pltpu.VMEM((n_image, 8, atoms), F32),
        dma((12,)), dma((12,)),
        dma((n_space,)), dma((n_space,)),
        dma((n_space,)), dma((n_space,)),
        dma((n_image,)), dma((n_image,)),
    ]
    new_pos, new_vel, energy = pl.pallas_call(
        functools.partial(body, n_space, n_image),
        out_shape=(
            jax.ShapeDtypeStruct(positions.shape, F32),
            jax.ShapeDtypeStruct(velocity.shape, F32),
            jax.ShapeDtypeStruct((1, 1), F32),
        ),
        in_specs=[vmem] * 6 + [smem] * 2 + [vmem] * 4 + [smem] * 3,
        out_specs=(vmem, vmem, vmem),
        scratch_shapes=scratch,
        compiler_params=pltpu.CompilerParams(
            collective_id=0, has_side_effects=True, vmem_limit_bytes=48 * 1024 * 1024
        ),
    )(
        positions, velocity, embed, neighbours, send_up.reshape(1, -1), send_down.reshape(1, -1),
        climb, reset, filter_in, filter_out, update_weight, readout.reshape(1, -1),
        spring.reshape(1, 1), time_step.reshape(1, 1), mixing.reshape(1, 1),
    )
    return new_pos, new_vel, energy.reshape(1)


def solution(mesh):
    placed = (
        P("image", None, "space"), P("image", None, "space"), P("space", None), P("space", None),
        P("space"), P("space"), P("image"), P("image"), P(), P(), P(), P(), P(), P(), P(),
    )
    return jax.shard_map(
        functools.partial(per_device, mesh.shape["space"], mesh.shape["image"]),
        mesh=mesh,
        in_specs=placed,
        out_specs=(P("image", None, "space"), P("image", None, "space"), P("image")),
        check_vma=False,
    )
```

```python
import functools
import jax
import jax.numpy as jnp
from jax import lax
from jax.experimental import pallas as pl
from jax.experimental.pallas import tpu as pltpu
from jax.sharding import PartitionSpec as P

EPSILON = 1e-06
BASIS_WIDTH = 0.6
BASIS_REACH = 6.0
F32 = jnp.float32
BF16 = jnp.bfloat16
MESH = pl.DeviceIdType.MESH


def dot(left, right):
    return jnp.dot(left, right, preferred_element_type=F32)


def dot_nt(left, right):
    return lax.dot_general(left, right, (((1,), (1,)), ((), ())), preferred_element_type=F32)


def dot_tn(left, right):
    return lax.dot_general(left, right, (((0,), (0,)), ((), ())), preferred_element_type=F32)


def gate(values):
    return 0.5 * jnp.tanh(0.5 * values) + 0.5


def split_two(values):
    high = values.astype(BF16)
    low = (values - high.astype(F32)).astype(BF16)
    return high, low


def onehot(mask):
    return jnp.where(mask, 1.0, 0.0).astype(BF16)


def body(
    n_space, n_image,
    pos_hbm, vel_hbm, emb_hbm, nb_hbm, up_hbm, down_hbm, climb_hbm, reset_hbm,
    fin_hbm, fout_hbm, uw_hbm, read_hbm, spring_hbm, step_hbm, mix_hbm,
    newpos_ref, newvel_ref, energy_ref,
    pos_ref, vel_ref, emb_ref, nb_t, up_ref, down_ref, climb_ref, reset_ref,
    fin_ref, fout_ref, uw_ref, read_ref, spring_ref, step_ref, mix_ref, fetch_sem,
    pos8, prev8, next8, coord, coord_src, ext_emb, emb_src, ext_hid, hid_src,
    grad_all, grad_src, grad_in, force_src, force_in,
    sel, sel_t, oh, oht, pv_all, slope_all, pre_two, ds_one, ds_two,
    rows_one, rows_two, filt_two, drad, w_in, w_back,
    norm_src, norm_in, sum_src, sum_in, band_src, band_in,
    send, recv, norm_send, norm_recv, sum_send, sum_recv, band_send, band_recv,
):
    domain = lax.axis_index("space")
    image = lax.axis_index("image")
    upper = lax.rem(domain + 1, n_space)
    lower = lax.rem(domain + n_space - 1, n_space)
    following = lax.rem(image + 1, n_image)
    previous = lax.rem(image + n_image - 1, n_image)
    per_atom, atoms = nb_t.shape
    ext = 3 * atoms
    chunks, pairs = oh.shape[0], oh.shape[1]
    basis = fin_ref.shape[1]
    channels = emb_ref.shape[1]

    sources = (
        pos_hbm, vel_hbm, emb_hbm, nb_hbm, up_hbm, down_hbm, climb_hbm, reset_hbm,
        fin_hbm, fout_hbm, uw_hbm, read_hbm, spring_hbm, step_hbm, mix_hbm,
    )
    targets = (
        pos_ref, vel_ref, emb_ref, nb_t, up_ref, down_ref, climb_ref, reset_ref,
        fin_ref, fout_ref, uw_ref, read_ref, spring_ref, step_ref, mix_ref,
    )
    fetches = [
        pltpu.make_async_copy(source, target, fetch_sem.at[i])
        for i, (source, target) in enumerate(zip(sources, targets))
    ]
    for i in (0, 4, 5, 2, 3, 8, 9, 10, 1, 11, 6, 7, 12, 13, 14):
        fetches[i].start()

    barrier = pltpu.get_barrier_semaphore()
    for i in range(1, n_space):
        pl.semaphore_signal(
            barrier, inc=1, device_id={"space": lax.rem(domain + i, n_space)}, device_id_type=MESH
        )
    for i in range(1, n_image):
        pl.semaphore_signal(
            barrier, inc=1, device_id={"image": lax.rem(image + i, n_image)}, device_id_type=MESH
        )

    def remote(src, dst, slot, where):
        return pltpu.make_async_remote_copy(
            src_ref=src, dst_ref=dst, send_sem=send.at[slot], recv_sem=recv.at[slot],
            device_id=where, device_id_type=MESH,
        )

    def spread(src, dst, out_sem, in_sem, axis, me, count):
        copies = []
        for i in range(1, count):
            copies.append(
                pltpu.make_async_remote_copy(
                    src_ref=src, dst_ref=dst.at[me], send_sem=out_sem.at[i], recv_sem=in_sem.at[me],
                    device_id={axis: lax.rem(me + i, count)}, device_id_type=MESH,
                )
            )
        for copy in copies:
            copy.start()
        dst[me] = src[...]

        def finish():
            for i in range(1, count):
                other = lax.rem(me + i, count)
                pltpu.make_async_remote_copy(
                    src_ref=src, dst_ref=dst.at[other], send_sem=out_sem.at[i],
                    recv_sem=in_sem.at[other], device_id={axis: other}, device_id_type=MESH,
                ).wait_recv()
            for copy in copies:
                copy.wait_send()

        return finish

    for i in (0, 4, 5, 2):
        fetches[i].wait()
    pos8[...] = jnp.zeros_like(pos8)
    for r in range(3):
        pos8[r : r + 1, :] = pos_ref[r]
    here = pos8[...]
    part_a = here.astype(BF16).astype(F32)
    rest = here - part_a
    part_b = rest.astype(BF16).astype(F32)
    part_c = rest - part_b
    parts = jnp.concatenate([part_a, part_b, part_c, jnp.zeros_like(here)], axis=0).astype(BF16)
    coord[0] = parts
    atom_rows = lax.broadcasted_iota(jnp.int32, (atoms, atoms), 0)
    embed = emb_ref[...]
    ext_emb[0:atoms, :] = embed
    for side, ids in ((0, up_ref), (1, down_ref)):
        picked = jnp.where(atom_rows == ids[...], 1.0, 0.0)
        sel_t[side] = picked.astype(BF16)
        sel[side] = picked.T.astype(BF16)
        coord_src[side] = dot(parts, sel_t[side]).astype(BF16)
        emb_src[side] = dot(sel[side], embed).astype(BF16)

    pl.semaphore_wait(barrier, n_space + n_image - 2)
    to_up, to_down = {"space": upper}, {"space": lower}
    coord_copies = [
        remote(coord_src.at[0], coord.at[1], 0, to_up),
        remote(coord_src.at[1], coord.at[2], 1, to_down),
    ]
    emb_copies = [
        remote(emb_src.at[0], ext_emb.at[pl.ds(atoms, atoms)], 2, to_up),
        remote(emb_src.at[1], ext_emb.at[pl.ds(2 * atoms, atoms)], 3, to_down),
    ]
    image_copies = [
        remote(pos8, prev8, 4, {"image": following}),
        remote(pos8, next8, 5, {"image": previous}),
    ]
    for copy in coord_copies + emb_copies + image_copies:
        copy.start()

    for i in (3, 8, 9, 10, 1, 11, 6, 7, 12, 13, 14):
        fetches[i].wait()
    nb = nb_t[...].T
    ext_lane = lax.broadcasted_iota(jnp.int32, (atoms, ext), 1)
    ext_row = lax.broadcasted_iota(jnp.int32, (ext, pairs), 0)
    per_chunk = pairs // atoms
    for k in range(per_atom):
        c, r = k // per_chunk, k % per_chunk
        oh[c, r * atoms : (r + 1) * atoms, :] = onehot(nb[:, k : k + 1] == ext_lane)

    def slot_row(c):
        return jnp.concatenate(
            [nb_t[pl.ds(c * per_chunk + r, 1), :] for r in range(per_chunk)], axis=1
        )

    def build(c, carry):
        oht[c] = onehot(slot_row(c) == ext_row)
        return carry

    lax.fori_loop(0, chunks, build, 0, unroll=2)
    for layer in range(2):
        high, low = split_two(fin_ref[layer])
        lanes = slice(layer * channels, (layer + 1) * channels)
        w_in[:, lanes] = jnp.concatenate([high, high, low], axis=0)
        w_back[layer] = jnp.concatenate([high, low], axis=0)

    for copy in coord_copies + emb_copies:
        copy.wait_recv()

    low_shift = jnp.where(domain == 0, -n_space, 0).astype(F32)
    high_shift = jnp.where(domain == n_space - 1, n_space, 0).astype(F32)
    all_coord = jnp.concatenate([coord[0], coord[1], coord[2]], axis=1)
    here_wide = jnp.concatenate([here] * per_chunk, axis=1)
    first_row = lax.broadcasted_iota(jnp.int32, (8, pairs), 0) == 0
    centres = lax.broadcasted_iota(jnp.int32, (basis, pairs), 0).astype(F32) * (
        BASIS_REACH / (basis - 1)
    )
    ext_embed = ext_emb[...]
    fout_one, fout_two = fout_ref[0], fout_ref[1]

    def fold(values):
        total = values[0:atoms]
        for r in range(1, per_chunk):
            total = total + values[r * atoms : (r + 1) * atoms]
        return total

    def repeat(values):
        return jnp.concatenate([values] * per_chunk, axis=0)

    def layer_one(c, total):
        found = dot(all_coord, oht[c])
        slots = slot_row(c)
        shift = jnp.where(
            slots >= 2 * atoms, high_shift, jnp.where(slots >= atoms, low_shift, 0.0)
        )
        there = found[0:8] + found[8:16] + found[16:24]
        vec = there + jnp.where(first_row, shift, 0.0) - here_wide
        pv_all[c] = vec
        sq_dist = jnp.sum(vec * vec, axis=0, keepdims=True)
        scaled = (sq_dist - centres) * (1.0 / BASIS_WIDTH)
        radial = jnp.exp(-scaled * scaled)
        slope_all[c] = radial * (-2.0 / BASIS_WIDTH) * scaled
        high, low = split_two(radial)
        pre = dot_tn(jnp.concatenate([high, low, high], axis=0), w_in[...])
        pre_two[c] = pre[:, channels:]
        pre_one = pre[:, :channels]
        sig = gate(pre_one)
        act = pre_one * sig
        ds_one[c] = (sig + act * (1.0 - sig)).astype(BF16)
        filt = dot(act.astype(BF16), fout_one)
        rows = dot(oh[c], ext_embed)
        rows_one[c] = rows.astype(BF16)
        return total + fold(filt * rows)

    zeros = jnp.zeros((atoms, channels), F32)
    msg_one = lax.fori_loop(0, chunks, layer_one, zeros, unroll=4)
    upd_one = dot(msg_one.astype(BF16), uw_ref[0])
    sig_one = gate(upd_one)
    act_one = upd_one * sig_one
    slope_one = sig_one + act_one * (1.0 - sig_one)
    hidden = (embed.astype(F32) + act_one).astype(BF16)
    ext_hid[0:atoms, :] = hidden
    hid_src[0] = dot(sel[0], hidden).astype(BF16)
    hid_src[1] = dot(sel[1], hidden).astype(BF16)
    hid_copies = [
        remote(hid_src.at[0], ext_hid.at[pl.ds(atoms, atoms)], 6, to_up),
        remote(hid_src.at[1], ext_hid.at[pl.ds(2 * atoms, atoms)], 7, to_down),
    ]
    for copy in hid_copies:
        copy.start()

    for copy in image_copies:
        copy.wait_recv()
    ahead = jnp.where(image == n_image - 1, 0.0, next8[...]) - here
    behind = here - jnp.where(image == 0, 0.0, prev8[...])
    row8 = lax.broadcasted_iota(jnp.int32, (8, atoms), 0)

    def place(values):
        block = jnp.zeros((8, atoms), F32)
        for r, value in enumerate(values):
            block = jnp.where(row8 == r, value, block)
        return block

    def rows_sum(values):
        return jnp.sum(values, axis=0, keepdims=True)

    norm_src[...] = place([rows_sum(ahead * ahead), rows_sum(behind * behind)])
    norm_done = spread(norm_src, norm_in, norm_send, norm_recv, "space", domain, n_space)

    def filter_two(c, carry):
        pre = pre_two[c]
        sig = gate(pre)
        act = pre * sig
        ds_two[c] = (sig + act * (1.0 - sig)).astype(BF16)
        filt_two[c] = dot(act.astype(BF16), fout_two)
        return carry

    lax.fori_loop(0, chunks, filter_two, 0, unroll=4)
    for copy in hid_copies:
        copy.wait_recv()
    ext_hidden = ext_hid[...]

    def layer_two(c, total):
        rows = dot(oh[c], ext_hidden)
        rows_two[c] = rows.astype(BF16)
        return total + fold(filt_two[c] * rows)

    msg_two = lax.fori_loop(0, chunks, layer_two, zeros, unroll=4)
    upd_two = dot(msg_two.astype(BF16), uw_ref[1])
    sig_two = gate(upd_two)
    act_two = upd_two * sig_two
    readout = read_ref[...]
    energy_row = rows_sum(act_two * readout)
    dupd_two = ((sig_two + act_two * (1.0 - sig_two)) * readout).astype(BF16)
    dmsg_two = dot_nt(dupd_two, uw_ref[1])

    grad_all[...] = jnp.zeros_like(grad_all)
    group = 4

    def scatter_two(g, carry):
        picks, sources = [], []
        for i in range(group):
            c = g * group + i
            picks.append(oht[c])
            sources.append((filt_two[c] * repeat(dmsg_two)).astype(BF16))
        grad_all[...] += dot(
            jnp.concatenate(picks, axis=1), jnp.concatenate(sources, axis=0)
        )
        return carry

    lax.fori_loop(0, chunks // group, scatter_two, 0)
    grad_src[0] = grad_all[atoms : 2 * atoms, :].astype(BF16)
    grad_src[1] = grad_all[2 * atoms : 3 * atoms, :].astype(BF16)
    grad_copies = [
        remote(grad_src.at[0], grad_in.at[0], 8, to_down),
        remote(grad_src.at[1], grad_in.at[1], 9, to_up),
    ]
    for copy in grad_copies:
        copy.start()

    def back(dmsg, rows, weight, slope, layer):
        dfilt = (repeat(dmsg) * rows.astype(F32)).astype(BF16)
        dact = dot_nt(dfilt, weight)
        dpre = (dact * slope.astype(F32)).astype(BF16)
        both = dot_nt(w_back[layer], dpre)
        return both[:basis] + both[basis:]

    def back_two(c, carry):
        drad[c] = back(dmsg_two, rows_two[c], fout_two, ds_two[c], 1)
        return carry

    lax.fori_loop(0, chunks, back_two, 0, unroll=4)
    for copy in grad_copies:
        copy.wait_recv()
    dhidden = grad_all[0:atoms, :] + dot(sel_t[0], grad_in[0]) + dot(sel_t[1], grad_in[1])
    dupd_one = (dhidden * slope_one).astype(BF16)
    dmsg_one = dot_nt(dupd_one, uw_ref[0])

    def back_one(c, carry):
        own, scattered = carry
        dradial = drad[c] + back(dmsg_one, rows_one[c], fout_one, ds_one[c], 0)
        dsq = jnp.sum(dradial * slope_all[c], axis=0, keepdims=True)
        pair = (2.0 * dsq) * pv_all[c]
        for r in range(per_chunk):
            own = own + pair[:, r * atoms : (r + 1) * atoms]
        high = pair.astype(BF16).astype(F32)
        both = jnp.concatenate([high, pair - high], axis=0).astype(BF16)
        return own, scattered + dot(both, oh[c])

    own, scattered = lax.fori_loop(
        0, chunks, back_one, (jnp.zeros((8, atoms), F32), jnp.zeros((16, ext), F32)),
        unroll=4,
    )
    scattered = scattered[0:8] + scattered[8:16]
    force_src[0] = scattered[:, atoms : 2 * atoms]
    force_src[1] = scattered[:, 2 * atoms : 3 * atoms]
    force_copies = [
        remote(force_src.at[0], force_in.at[0], 10, to_down),
        remote(force_src.at[1], force_in.at[1], 11, to_up),
    ]
    for copy in force_copies:
        copy.start()

    norm_done()
    norm_sum = norm_in[0]
    for i in range(1, n_space):
        norm_sum = norm_sum + norm_in[i]
    norms = jnp.sqrt(jnp.sum(norm_sum, axis=1, keepdims=True) + EPSILON)
    ahead_norm, behind_norm = norms[0:1], norms[1:2]
    tangent = ahead / ahead_norm + behind / behind_norm
    tangent_row = rows_sum(tangent * tangent)
    speed = place([vel_ref[r] for r in range(3)])
    speed_row = rows_sum(speed * speed)
    spring_part = spring_ref[0] * (ahead_norm - behind_norm)
    local_force = own - scattered[:, 0:atoms]
    for copy in force_copies:
        copy.wait_recv()

    def returned(side):
        ghost = force_in[side]
        high = ghost.astype(BF16).astype(F32)
        both = dot(jnp.concatenate([high, ghost - high], axis=0).astype(BF16), sel[side])
        return both[0:8] + both[8:16]

    forces = local_force - returned(0) - returned(1)
    sum_src[...] = place(
        [
            rows_sum(forces * forces), rows_sum(forces * tangent), tangent_row, energy_row,
            speed_row,
        ]
    )
    sum_done = spread(sum_src, sum_in, sum_send, sum_recv, "space", domain, n_space)
    sum_done()
    sums = sum_in[0]
    for i in range(1, n_space):
        sums = sums + sum_in[i]
    sums = jnp.sum(sums, axis=1, keepdims=True)
    force_sq, along, tangent_sq = sums[0:1], sums[1:2], sums[2:3]
    energy_ref[...] = sums[3:4]
    scale = 1.0 / jnp.sqrt(tangent_sq + EPSILON)
    parallel = along * scale
    unit_sq = tangent_sq * scale * scale
    climbing = climb_ref[0] > 0
    take = jnp.where(climbing, 2.0 * parallel, parallel - spring_part)
    movable = jnp.where((image > 0) & (image < n_image - 1), 1.0, 0.0)
    band_sq = jnp.maximum(force_sq - 2.0 * take * parallel + take * take * unit_sq, 0.0)
    band_src[...] = place([band_sq * movable, sums[4:5] * movable])
    band_done = spread(band_src, band_in, band_send, band_recv, "image", image, n_image)
    band_force = (forces - take * (tangent * scale)) * movable
    band_done()
    totals = band_in[0]
    for i in range(1, n_image):
        totals = totals + band_in[i]
    totals = jnp.sqrt(totals + EPSILON)
    force_norm, speed_norm = totals[0:1], totals[1:2]
    mixing = mix_ref[0]
    time_step = step_ref[0]
    mixed = (1.0 - mixing) * speed + mixing * (speed_norm / force_norm) * band_force
    kept = jnp.where(reset_ref[0] > 0, 0.0, mixed)
    new_speed = (kept + time_step * band_force) * movable
    new_place = here + time_step * new_speed
    for r in range(3):
        newvel_ref[r] = new_speed[r : r + 1]
        newpos_ref[r] = new_place[r : r + 1]
    for copy in (
        coord_copies + emb_copies + image_copies + hid_copies + grad_copies + force_copies
    ):
        copy.wait_send()


def per_device(
    n_space, n_image,
    positions, velocity, embed, neighbours, send_up, send_down, climb, reset,
    filter_in, filter_out, update_weight, readout, spring, time_step, mixing,
):
    atoms, per_atom = neighbours.shape
    channels = embed.shape[1]
    basis = filter_in.shape[1]
    per_chunk = 2
    chunks, pairs = per_atom // per_chunk, per_chunk * atoms
    ext = 3 * atoms
    vmem = pl.BlockSpec(memory_space=pltpu.VMEM)
    hbm = pl.BlockSpec(memory_space=pltpu.HBM)
    dma = pltpu.SemaphoreType.DMA
    basis_shape = filter_in.shape
    scratch = [
        pltpu.VMEM((3, 1, atoms), F32),
        pltpu.VMEM((3, 1, atoms), F32),
        pltpu.VMEM((atoms, channels), BF16),
        pltpu.VMEM((per_atom, atoms), jnp.int32),
        pltpu.VMEM((1, atoms), jnp.int32),
        pltpu.VMEM((1, atoms), jnp.int32),
        pltpu.SMEM((1,), jnp.int32),
        pltpu.SMEM((1,), jnp.int32),
        pltpu.VMEM(basis_shape, F32),
        pltpu.VMEM((2, channels, channels), BF16),
        pltpu.VMEM((2, channels, channels), BF16),
        pltpu.VMEM((1, channels), F32),
        pltpu.SMEM((1,), F32),
        pltpu.SMEM((1,), F32),
        pltpu.SMEM((1,), F32),
        dma((15,)),
        pltpu.VMEM((8, atoms), F32),
        pltpu.VMEM((8, atoms), F32),
        pltpu.VMEM((8, atoms), F32),
        pltpu.VMEM((3, 32, atoms), BF16),
        pltpu.VMEM((2, 32, atoms), BF16),
        pltpu.VMEM((ext, channels), BF16),
        pltpu.VMEM((2, atoms, channels), BF16),
        pltpu.VMEM((ext, channels), BF16),
        pltpu.VMEM((2, atoms, channels), BF16),
        pltpu.VMEM((ext, channels), F32),
        pltpu.VMEM((2, atoms, channels), BF16),
        pltpu.VMEM((2, atoms, channels), BF16),
        pltpu.VMEM((2, 8, atoms), F32),
        pltpu.VMEM((2, 8, atoms), F32),
        pltpu.VMEM((2, atoms, atoms), BF16),
        pltpu.VMEM((2, atoms, atoms), BF16),
        pltpu.VMEM((chunks, pairs, ext), BF16),
        pltpu.VMEM((chunks, ext, pairs), BF16),
        pltpu.VMEM((chunks, 8, pairs), F32),
        pltpu.VMEM((chunks, basis, pairs), F32),
        pltpu.VMEM((chunks, pairs, channels), F32),
        pltpu.VMEM((chunks, pairs, channels), BF16),
        pltpu.VMEM((chunks, pairs, channels), BF16),
        pltpu.VMEM((chunks, pairs, channels), BF16),
        pltpu.VMEM((chunks, pairs, channels), BF16),
        pltpu.VMEM((chunks, pairs, channels), F32),
        pltpu.VMEM((chunks, basis, pairs), F32),
        pltpu.VMEM((3 * basis, 2 * channels), BF16),
        pltpu.VMEM((2, 2 * basis, channels), BF16),
        pltpu.VMEM((8, atoms), F32),
        pltpu.VMEM((n_space, 8, atoms), F32),
        pltpu.VMEM((8, atoms), F32),
        pltpu.VMEM((n_space, 8, atoms), F32),
        pltpu.VMEM((8, atoms), F32),
        pltpu.VMEM((n_image, 8, atoms), F32),
        dma((12,)), dma((12,)),
        dma((n_space,)), dma((n_space,)),
        dma((n_space,)), dma((n_space,)),
        dma((n_image,)), dma((n_image,)),
    ]
    new_pos, new_vel, energy = pl.pallas_call(
        functools.partial(body, n_space, n_image),
        out_shape=(
            jax.ShapeDtypeStruct((3, 1, atoms), F32),
            jax.ShapeDtypeStruct((3, 1, atoms), F32),
            jax.ShapeDtypeStruct((1, 1), F32),
        ),
        in_specs=[hbm] * 15,
        out_specs=(vmem, vmem, vmem),
        scratch_shapes=scratch,
        compiler_params=pltpu.CompilerParams(
            collective_id=0, has_side_effects=True, vmem_limit_bytes=60 * 1024 * 1024
        ),
    )(
        jnp.transpose(positions, (1, 0, 2)), jnp.transpose(velocity, (1, 0, 2)), embed,
        neighbours.T, send_up.reshape(1, -1), send_down.reshape(1, -1), climb, reset,
        filter_in, filter_out, update_weight, readout.reshape(1, -1),
        spring.reshape(1), time_step.reshape(1), mixing.reshape(1),
    )
    back = (1, 0, 2)
    return jnp.transpose(new_pos, back), jnp.transpose(new_vel, back), energy.reshape(1)


def solution(mesh):
    placed = (
        P("image", None, "space"), P("image", None, "space"), P("space", None), P("space", None),
        P("space"), P("space"), P("image"), P("image"), P(), P(), P(), P(), P(), P(), P(),
    )
    return jax.shard_map(
        functools.partial(per_device, mesh.shape["space"], mesh.shape["image"]),
        mesh=mesh,
        in_specs=placed,
        out_specs=(P("image", None, "space"), P("image", None, "space"), P("image")),
        check_vma=False,
    )
```

```python
import functools
import jax
import jax.numpy as jnp
from jax import lax
from jax.experimental import pallas as pl
from jax.experimental.pallas import tpu as pltpu
from jax.sharding import PartitionSpec as P

EPSILON = 1e-06
BASIS_WIDTH = 0.6
BASIS_REACH = 6.0
F32 = jnp.float32
BF16 = jnp.bfloat16
MESH = pl.DeviceIdType.MESH


def dot(left, right):
    return jnp.dot(left, right, preferred_element_type=F32)


def dot_nt(left, right):
    return lax.dot_general(left, right, (((1,), (1,)), ((), ())), preferred_element_type=F32)


def dot_tn(left, right):
    return lax.dot_general(left, right, (((0,), (0,)), ((), ())), preferred_element_type=F32)


def gate(values):
    return 0.5 * jnp.tanh(0.5 * values) + 0.5


def split_two(values):
    high = values.astype(BF16)
    low = (values - high.astype(F32)).astype(BF16)
    return high, low


def onehot(mask):
    return jnp.where(mask, 1.0, 0.0).astype(BF16)


def body(
    n_space, n_image,
    pos_hbm, vel_hbm, emb_hbm, nb_hbm, up_hbm, down_hbm, climb_hbm, reset_hbm,
    fin_hbm, fout_hbm, uw_hbm, read_hbm, spring_hbm, step_hbm, mix_hbm,
    newpos_ref, newvel_ref, energy_ref,
    pos_ref, vel_ref, emb_ref, nb_t, up_ref, down_ref, climb_ref, reset_ref,
    fin_ref, fout_ref, uw_ref, read_ref, spring_ref, step_ref, mix_ref, fetch_sem,
    pos8, prev8, next8, coord, coord_src, ext_emb, emb_src, ext_hid, hid_src,
    grad_all, grad_src, grad_in, force_src, force_in,
    sel, sel_t, oh, oht, pv_all, slope_all, pre_two, ds_one, ds_two,
    rows_one, rows_two, filt_two, drad, w_in, w_back,
    norm_src, norm_in, sum_src, sum_in, band_src, band_in,
    send, recv, norm_send, norm_recv, sum_send, sum_recv, band_send, band_recv,
):
    domain = lax.axis_index("space")
    image = lax.axis_index("image")
    upper = lax.rem(domain + 1, n_space)
    lower = lax.rem(domain + n_space - 1, n_space)
    following = lax.rem(image + 1, n_image)
    previous = lax.rem(image + n_image - 1, n_image)
    per_atom, atoms = nb_t.shape
    ext = 3 * atoms
    chunks, pairs = oh.shape[0], oh.shape[1]
    basis = fin_ref.shape[1]
    channels = emb_ref.shape[1]

    sources = (
        pos_hbm, vel_hbm, emb_hbm, nb_hbm, up_hbm, down_hbm, climb_hbm, reset_hbm,
        fin_hbm, fout_hbm, uw_hbm, read_hbm, spring_hbm, step_hbm, mix_hbm,
    )
    targets = (
        pos_ref, vel_ref, emb_ref, nb_t, up_ref, down_ref, climb_ref, reset_ref,
        fin_ref, fout_ref, uw_ref, read_ref, spring_ref, step_ref, mix_ref,
    )
    fetches = [
        pltpu.make_async_copy(source, target, fetch_sem.at[i])
        for i, (source, target) in enumerate(zip(sources, targets))
    ]
    for i in (0, 4, 5, 2, 3, 8, 9, 10, 1, 11, 6, 7, 12, 13, 14):
        fetches[i].start()

    barrier = pltpu.get_barrier_semaphore()
    for i in range(1, n_space):
        pl.semaphore_signal(
            barrier, inc=1, device_id={"space": lax.rem(domain + i, n_space)}, device_id_type=MESH
        )
    for i in range(1, n_image):
        pl.semaphore_signal(
            barrier, inc=1, device_id={"image": lax.rem(image + i, n_image)}, device_id_type=MESH
        )

    def remote(src, dst, slot, where):
        return pltpu.make_async_remote_copy(
            src_ref=src, dst_ref=dst, send_sem=send.at[slot], recv_sem=recv.at[slot],
            device_id=where, device_id_type=MESH,
        )

    def spread(src, dst, out_sem, in_sem, axis, me, count):
        copies = []
        for i in range(1, count):
            copies.append(
                pltpu.make_async_remote_copy(
                    src_ref=src, dst_ref=dst.at[me], send_sem=out_sem.at[i], recv_sem=in_sem.at[me],
                    device_id={axis: lax.rem(me + i, count)}, device_id_type=MESH,
                )
            )
        for copy in copies:
            copy.start()
        dst[me] = src[...]

        def finish():
            for i in range(1, count):
                other = lax.rem(me + i, count)
                pltpu.make_async_remote_copy(
                    src_ref=src, dst_ref=dst.at[other], send_sem=out_sem.at[i],
                    recv_sem=in_sem.at[other], device_id={axis: other}, device_id_type=MESH,
                ).wait_recv()
            for copy in copies:
                copy.wait_send()

        return finish

    for i in (0, 4, 5, 2):
        fetches[i].wait()
    pos8[...] = jnp.zeros_like(pos8)
    for r in range(3):
        pos8[r : r + 1, :] = pos_ref[r]
    here = pos8[...]
    part_a = here.astype(BF16).astype(F32)
    rest = here - part_a
    part_b = rest.astype(BF16).astype(F32)
    part_c = rest - part_b
    parts = jnp.concatenate([part_a, part_b, part_c, jnp.zeros_like(here)], axis=0).astype(BF16)
    coord[0] = parts
    atom_rows = lax.broadcasted_iota(jnp.int32, (atoms, atoms), 0)
    embed = emb_ref[...]
    ext_emb[0:atoms, :] = embed
    for side, ids in ((0, up_ref), (1, down_ref)):
        picked = jnp.where(atom_rows == ids[...], 1.0, 0.0)
        sel_t[side] = picked.astype(BF16)
        sel[side] = picked.T.astype(BF16)
        coord_src[side] = dot(parts, sel_t[side]).astype(BF16)
        emb_src[side] = dot(sel[side], embed).astype(BF16)

    fetches[3].wait()
    per_chunk = pairs // atoms
    ext_lane = lax.broadcasted_iota(jnp.int32, (atoms, ext), 1)
    nb_wide = jnp.concatenate(
        [nb_t[...], jnp.zeros((atoms - per_atom, atoms), jnp.int32)], axis=0
    ).T

    def build_rows(c, slots):
        for r in range(per_chunk):
            oh[c, r * atoms : (r + 1) * atoms, :] = onehot(slots[:, 0:1] == ext_lane)
            slots = pltpu.roll(slots, atoms - 1, 1)
        return slots

    lax.fori_loop(0, chunks, build_rows, nb_wide, unroll=2)
    pl.semaphore_wait(barrier, n_space + n_image - 2)
    to_up, to_down = {"space": upper}, {"space": lower}
    coord_copies = [
        remote(coord_src.at[0], coord.at[1], 0, to_up),
        remote(coord_src.at[1], coord.at[2], 1, to_down),
    ]
    emb_copies = [
        remote(emb_src.at[0], ext_emb.at[pl.ds(atoms, atoms)], 2, to_up),
        remote(emb_src.at[1], ext_emb.at[pl.ds(2 * atoms, atoms)], 3, to_down),
    ]
    image_copies = [
        remote(pos8, prev8, 4, {"image": following}),
        remote(pos8, next8, 5, {"image": previous}),
    ]
    for copy in coord_copies + emb_copies + image_copies:
        copy.start()

    for i in (8, 9, 10, 1, 11, 6, 7, 12, 13, 14):
        fetches[i].wait()
    ext_row = lax.broadcasted_iota(jnp.int32, (ext, pairs), 0)
    def slot_row(c):
        return jnp.concatenate(
            [nb_t[pl.ds(c * per_chunk + r, 1), :] for r in range(per_chunk)], axis=1
        )

    def build(c, carry):
        oht[c] = onehot(slot_row(c) == ext_row)
        return carry

    lax.fori_loop(0, chunks, build, 0, unroll=2)
    for layer in range(2):
        high, low = split_two(fin_ref[layer])
        lanes = slice(layer * channels, (layer + 1) * channels)
        w_in[:, lanes] = jnp.concatenate([high, high, low], axis=0)
        w_back[layer] = jnp.concatenate([high, low], axis=0)

    for copy in coord_copies + emb_copies:
        copy.wait_recv()

    low_shift = jnp.where(domain == 0, -n_space, 0).astype(F32)
    high_shift = jnp.where(domain == n_space - 1, n_space, 0).astype(F32)
    all_coord = jnp.concatenate([coord[0], coord[1], coord[2]], axis=1)
    here_wide = jnp.concatenate([here] * per_chunk, axis=1)
    first_row = lax.broadcasted_iota(jnp.int32, (8, pairs), 0) == 0
    centres = lax.broadcasted_iota(jnp.int32, (basis, pairs), 0).astype(F32) * (
        BASIS_REACH / (basis - 1)
    )
    ext_embed = ext_emb[...]
    fout_one, fout_two = fout_ref[0], fout_ref[1]

    def fold(values):
        total = values[0:atoms]
        for r in range(1, per_chunk):
            total = total + values[r * atoms : (r + 1) * atoms]
        return total

    def repeat(values):
        return jnp.concatenate([values] * per_chunk, axis=0)

    def layer_one(c, total):
        found = dot(all_coord, oht[c])
        slots = slot_row(c)
        shift = jnp.where(
            slots >= 2 * atoms, high_shift, jnp.where(slots >= atoms, low_shift, 0.0)
        )
        there = found[0:8] + found[8:16] + found[16:24]
        vec = there + jnp.where(first_row, shift, 0.0) - here_wide
        pv_all[c] = vec
        sq_dist = jnp.sum(vec * vec, axis=0, keepdims=True)
        scaled = (sq_dist - centres) * (1.0 / BASIS_WIDTH)
        radial = jnp.exp(-scaled * scaled)
        slope_all[c] = radial * (-2.0 / BASIS_WIDTH) * scaled
        high, low = split_two(radial)
        pre = dot_tn(jnp.concatenate([high, low, high], axis=0), w_in[...])
        pre_two[c] = pre[:, channels:]
        pre_one = pre[:, :channels]
        sig = gate(pre_one)
        act = pre_one * sig
        sig, act = sig.astype(BF16), act.astype(BF16)
        ds_one[c] = sig + act * (1.0 - sig)
        filt = dot(act, fout_one)
        rows = dot(oh[c], ext_embed)
        rows_one[c] = rows.astype(BF16)
        return total + fold(filt * rows)

    zeros = jnp.zeros((atoms, channels), F32)
    msg_one = lax.fori_loop(0, chunks, layer_one, zeros, unroll=4)
    upd_one = dot(msg_one.astype(BF16), uw_ref[0])
    sig_one = gate(upd_one)
    act_one = upd_one * sig_one
    slope_one = sig_one + act_one * (1.0 - sig_one)
    hidden = (embed.astype(F32) + act_one).astype(BF16)
    ext_hid[0:atoms, :] = hidden
    hid_src[0] = dot(sel[0], hidden).astype(BF16)
    hid_src[1] = dot(sel[1], hidden).astype(BF16)
    hid_copies = [
        remote(hid_src.at[0], ext_hid.at[pl.ds(atoms, atoms)], 6, to_up),
        remote(hid_src.at[1], ext_hid.at[pl.ds(2 * atoms, atoms)], 7, to_down),
    ]
    for copy in hid_copies:
        copy.start()

    for copy in image_copies:
        copy.wait_recv()
    ahead = jnp.where(image == n_image - 1, 0.0, next8[...]) - here
    behind = here - jnp.where(image == 0, 0.0, prev8[...])
    row8 = lax.broadcasted_iota(jnp.int32, (8, atoms), 0)

    def place(values):
        block = jnp.zeros((8, atoms), F32)
        for r, value in enumerate(values):
            block = jnp.where(row8 == r, value, block)
        return block

    def rows_sum(values):
        return jnp.sum(values, axis=0, keepdims=True)

    norm_src[...] = place([rows_sum(ahead * ahead), rows_sum(behind * behind)])
    norm_done = spread(norm_src, norm_in, norm_send, norm_recv, "space", domain, n_space)

    def filter_two(c, carry):
        pre = pre_two[c]
        sig = gate(pre)
        act = pre * sig
        sig, act = sig.astype(BF16), act.astype(BF16)
        ds_two[c] = sig + act * (1.0 - sig)
        filt_two[c] = dot(act, fout_two)
        return carry

    lax.fori_loop(0, chunks, filter_two, 0, unroll=8)
    for copy in hid_copies:
        copy.wait_recv()
    ext_hidden = ext_hid[...]

    def layer_two(c, total):
        rows = dot(oh[c], ext_hidden)
        rows_two[c] = rows.astype(BF16)
        return total + fold(filt_two[c] * rows)

    msg_two = lax.fori_loop(0, chunks, layer_two, zeros, unroll=8)
    upd_two = dot(msg_two.astype(BF16), uw_ref[1])
    sig_two = gate(upd_two)
    act_two = upd_two * sig_two
    readout = read_ref[...]
    energy_row = rows_sum(act_two * readout)
    dupd_two = ((sig_two + act_two * (1.0 - sig_two)) * readout).astype(BF16)
    dmsg_two = dot_nt(dupd_two, uw_ref[1])

    grad_all[...] = jnp.zeros_like(grad_all)
    group = 4

    def scatter_two(g, carry):
        picks, sources = [], []
        for i in range(group):
            c = g * group + i
            picks.append(oht[c])
            sources.append((filt_two[c] * repeat(dmsg_two)).astype(BF16))
        grad_all[...] += dot(
            jnp.concatenate(picks, axis=1), jnp.concatenate(sources, axis=0)
        )
        return carry

    lax.fori_loop(0, chunks // group, scatter_two, 0)
    grad_src[0] = grad_all[atoms : 2 * atoms, :].astype(BF16)
    grad_src[1] = grad_all[2 * atoms : 3 * atoms, :].astype(BF16)
    grad_copies = [
        remote(grad_src.at[0], grad_in.at[0], 8, to_down),
        remote(grad_src.at[1], grad_in.at[1], 9, to_up),
    ]
    for copy in grad_copies:
        copy.start()

    def back(dmsg, rows, weight, slope, layer):
        dact = dot_nt(repeat(dmsg) * rows, weight)
        dpre = dact.astype(BF16) * slope
        both = dot_nt(w_back[layer], dpre)
        return both[:basis] + both[basis:]

    def back_two(c, carry):
        drad[c] = back(dmsg_two_low, rows_two[c], fout_two, ds_two[c], 1)
        return carry

    dmsg_two_low = dmsg_two.astype(BF16)
    lax.fori_loop(0, chunks, back_two, 0, unroll=8)
    for copy in grad_copies:
        copy.wait_recv()
    dhidden = grad_all[0:atoms, :] + dot(sel_t[0], grad_in[0]) + dot(sel_t[1], grad_in[1])
    dupd_one = (dhidden * slope_one).astype(BF16)
    dmsg_one = dot_nt(dupd_one, uw_ref[0]).astype(BF16)

    def back_one(c, carry):
        own, scattered = carry
        dradial = drad[c] + back(dmsg_one, rows_one[c], fout_one, ds_one[c], 0)
        dsq = jnp.sum(dradial * slope_all[c], axis=0, keepdims=True)
        pair = (2.0 * dsq) * pv_all[c]
        for r in range(per_chunk):
            own = own + pair[:, r * atoms : (r + 1) * atoms]
        high = pair.astype(BF16).astype(F32)
        both = jnp.concatenate([high, pair - high], axis=0).astype(BF16)
        return own, scattered + dot(both, oh[c])

    own, scattered = lax.fori_loop(
        0, chunks, back_one, (jnp.zeros((8, atoms), F32), jnp.zeros((16, ext), F32)),
        unroll=4,
    )
    scattered = scattered[0:8] + scattered[8:16]
    force_src[0] = scattered[:, atoms : 2 * atoms]
    force_src[1] = scattered[:, 2 * atoms : 3 * atoms]
    force_copies = [
        remote(force_src.at[0], force_in.at[0], 10, to_down),
        remote(force_src.at[1], force_in.at[1], 11, to_up),
    ]
    for copy in force_copies:
        copy.start()

    norm_done()
    norm_sum = norm_in[0]
    for i in range(1, n_space):
        norm_sum = norm_sum + norm_in[i]
    norms = jnp.sqrt(jnp.sum(norm_sum, axis=1, keepdims=True) + EPSILON)
    ahead_norm, behind_norm = norms[0:1], norms[1:2]
    tangent = ahead / ahead_norm + behind / behind_norm
    tangent_row = rows_sum(tangent * tangent)
    speed = place([vel_ref[r] for r in range(3)])
    speed_row = rows_sum(speed * speed)
    spring_part = spring_ref[0] * (ahead_norm - behind_norm)
    local_force = own - scattered[:, 0:atoms]
    for copy in force_copies:
        copy.wait_recv()

    def returned(side):
        ghost = force_in[side]
        high = ghost.astype(BF16).astype(F32)
        both = dot(jnp.concatenate([high, ghost - high], axis=0).astype(BF16), sel[side])
        return both[0:8] + both[8:16]

    forces = local_force - returned(0) - returned(1)
    sum_src[...] = place(
        [
            rows_sum(forces * forces), rows_sum(forces * tangent), tangent_row, energy_row,
            speed_row,
        ]
    )
    sum_done = spread(sum_src, sum_in, sum_send, sum_recv, "space", domain, n_space)
    sum_done()
    sums = sum_in[0]
    for i in range(1, n_space):
        sums = sums + sum_in[i]
    sums = jnp.sum(sums, axis=1, keepdims=True)
    force_sq, along, tangent_sq = sums[0:1], sums[1:2], sums[2:3]
    energy_ref[...] = sums[3:4]
    scale = 1.0 / jnp.sqrt(tangent_sq + EPSILON)
    parallel = along * scale
    unit_sq = tangent_sq * scale * scale
    climbing = climb_ref[0] > 0
    take = jnp.where(climbing, 2.0 * parallel, parallel - spring_part)
    movable = jnp.where((image > 0) & (image < n_image - 1), 1.0, 0.0)
    band_sq = jnp.maximum(force_sq - 2.0 * take * parallel + take * take * unit_sq, 0.0)
    band_src[...] = place([band_sq * movable, sums[4:5] * movable])
    band_done = spread(band_src, band_in, band_send, band_recv, "image", image, n_image)
    band_force = (forces - take * (tangent * scale)) * movable
    band_done()
    totals = band_in[0]
    for i in range(1, n_image):
        totals = totals + band_in[i]
    totals = jnp.sqrt(totals + EPSILON)
    force_norm, speed_norm = totals[0:1], totals[1:2]
    mixing = mix_ref[0]
    time_step = step_ref[0]
    mixed = (1.0 - mixing) * speed + mixing * (speed_norm / force_norm) * band_force
    kept = jnp.where(reset_ref[0] > 0, 0.0, mixed)
    new_speed = (kept + time_step * band_force) * movable
    new_place = here + time_step * new_speed
    for r in range(3):
        newvel_ref[r] = new_speed[r : r + 1]
        newpos_ref[r] = new_place[r : r + 1]
    for copy in (
        coord_copies + emb_copies + image_copies + hid_copies + grad_copies + force_copies
    ):
        copy.wait_send()


def per_device(
    n_space, n_image,
    positions, velocity, embed, neighbours, send_up, send_down, climb, reset,
    filter_in, filter_out, update_weight, readout, spring, time_step, mixing,
):
    atoms, per_atom = neighbours.shape
    channels = embed.shape[1]
    basis = filter_in.shape[1]
    per_chunk = 2
    chunks, pairs = per_atom // per_chunk, per_chunk * atoms
    ext = 3 * atoms
    vmem = pl.BlockSpec(memory_space=pltpu.VMEM)
    hbm = pl.BlockSpec(memory_space=pltpu.HBM)
    dma = pltpu.SemaphoreType.DMA
    basis_shape = filter_in.shape
    scratch = [
        pltpu.VMEM((3, 1, atoms), F32),
        pltpu.VMEM((3, 1, atoms), F32),
        pltpu.VMEM((atoms, channels), BF16),
        pltpu.VMEM((per_atom, atoms), jnp.int32),
        pltpu.VMEM((1, atoms), jnp.int32),
        pltpu.VMEM((1, atoms), jnp.int32),
        pltpu.SMEM((1,), jnp.int32),
        pltpu.SMEM((1,), jnp.int32),
        pltpu.VMEM(basis_shape, F32),
        pltpu.VMEM((2, channels, channels), BF16),
        pltpu.VMEM((2, channels, channels), BF16),
        pltpu.VMEM((1, channels), F32),
        pltpu.SMEM((1,), F32),
        pltpu.SMEM((1,), F32),
        pltpu.SMEM((1,), F32),
        dma((15,)),
        pltpu.VMEM((8, atoms), F32),
        pltpu.VMEM((8, atoms), F32),
        pltpu.VMEM((8, atoms), F32),
        pltpu.VMEM((3, 32, atoms), BF16),
        pltpu.VMEM((2, 32, atoms), BF16),
        pltpu.VMEM((ext, channels), BF16),
        pltpu.VMEM((2, atoms, channels), BF16),
        pltpu.VMEM((ext, channels), BF16),
        pltpu.VMEM((2, atoms, channels), BF16),
        pltpu.VMEM((ext, channels), F32),
        pltpu.VMEM((2, atoms, channels), BF16),
        pltpu.VMEM((2, atoms, channels), BF16),
        pltpu.VMEM((2, 8, atoms), F32),
        pltpu.VMEM((2, 8, atoms), F32),
        pltpu.VMEM((2, atoms, atoms), BF16),
        pltpu.VMEM((2, atoms, atoms), BF16),
        pltpu.VMEM((chunks, pairs, ext), BF16),
        pltpu.VMEM((chunks, ext, pairs), BF16),
        pltpu.VMEM((chunks, 8, pairs), F32),
        pltpu.VMEM((chunks, basis, pairs), F32),
        pltpu.VMEM((chunks, pairs, channels), F32),
        pltpu.VMEM((chunks, pairs, channels), BF16),
        pltpu.VMEM((chunks, pairs, channels), BF16),
        pltpu.VMEM((chunks, pairs, channels), BF16),
        pltpu.VMEM((chunks, pairs, channels), BF16),
        pltpu.VMEM((chunks, pairs, channels), F32),
        pltpu.VMEM((chunks, basis, pairs), F32),
        pltpu.VMEM((3 * basis, 2 * channels), BF16),
        pltpu.VMEM((2, 2 * basis, channels), BF16),
        pltpu.VMEM((8, atoms), F32),
        pltpu.VMEM((n_space, 8, atoms), F32),
        pltpu.VMEM((8, atoms), F32),
        pltpu.VMEM((n_space, 8, atoms), F32),
        pltpu.VMEM((8, atoms), F32),
        pltpu.VMEM((n_image, 8, atoms), F32),
        dma((12,)), dma((12,)),
        dma((n_space,)), dma((n_space,)),
        dma((n_space,)), dma((n_space,)),
        dma((n_image,)), dma((n_image,)),
    ]
    new_pos, new_vel, energy = pl.pallas_call(
        functools.partial(body, n_space, n_image),
        out_shape=(
            jax.ShapeDtypeStruct((3, 1, atoms), F32),
            jax.ShapeDtypeStruct((3, 1, atoms), F32),
            jax.ShapeDtypeStruct((1, 1), F32),
        ),
        in_specs=[hbm] * 15,
        out_specs=(vmem, vmem, vmem),
        scratch_shapes=scratch,
        compiler_params=pltpu.CompilerParams(
            collective_id=0, has_side_effects=True, vmem_limit_bytes=60 * 1024 * 1024
        ),
    )(
        jnp.transpose(positions, (1, 0, 2)), jnp.transpose(velocity, (1, 0, 2)), embed,
        neighbours.T, send_up.reshape(1, -1), send_down.reshape(1, -1), climb, reset,
        filter_in, filter_out, update_weight, readout.reshape(1, -1),
        spring.reshape(1), time_step.reshape(1), mixing.reshape(1),
    )
    back = (1, 0, 2)
    return jnp.transpose(new_pos, back), jnp.transpose(new_vel, back), energy.reshape(1)


def solution(mesh):
    placed = (
        P("image", None, "space"), P("image", None, "space"), P("space", None), P("space", None),
        P("space"), P("space"), P("image"), P("image"), P(), P(), P(), P(), P(), P(), P(),
    )
    return jax.shard_map(
        functools.partial(per_device, mesh.shape["space"], mesh.shape["image"]),
        mesh=mesh,
        in_specs=placed,
        out_specs=(P("image", None, "space"), P("image", None, "space"), P("image")),
        check_vma=False,
    )
```

```python
import functools
import jax
import jax.numpy as jnp
from jax import lax
from jax.experimental import pallas as pl
from jax.experimental.pallas import tpu as pltpu
from jax.sharding import PartitionSpec as P

EPSILON = 1e-06
BASIS_WIDTH = 0.6
BASIS_REACH = 6.0
F32 = jnp.float32
BF16 = jnp.bfloat16
MESH = pl.DeviceIdType.MESH


def dot(left, right):
    return jnp.dot(left, right, preferred_element_type=F32)


def dot_nt(left, right):
    return lax.dot_general(left, right, (((1,), (1,)), ((), ())), preferred_element_type=F32)


def dot_tn(left, right):
    return lax.dot_general(left, right, (((0,), (0,)), ((), ())), preferred_element_type=F32)


def gate(values):
    return 0.5 * jnp.tanh(0.5 * values) + 0.5


def split_two(values):
    high = values.astype(BF16)
    low = (values - high.astype(F32)).astype(BF16)
    return high, low


def onehot(mask):
    return jnp.where(mask, 1.0, 0.0).astype(BF16)


def body(
    n_space, n_image,
    pos_hbm, vel_hbm, emb_hbm, nb_hbm, up_hbm, down_hbm, climb_hbm, reset_hbm,
    fin_hbm, fout_hbm, uw_hbm, read_hbm, spring_hbm, step_hbm, mix_hbm,
    newpos_ref, newvel_ref, energy_ref,
    pos_ref, vel_ref, emb_ref, nb_t, up_ref, down_ref, climb_ref, reset_ref,
    fin_ref, fout_ref, uw_ref, read_ref, spring_ref, step_ref, mix_ref, fetch_sem,
    pos8, prev8, next8, coord, coord_src, ext_emb, emb_src, ext_hid, hid_src,
    grad_all, grad_src, grad_in, force_src, force_in,
    sel, sel_t, oh, oht, pv_all, slope_all, pre_two, ds_one, ds_two,
    rows_one, rows_two, filt_two, drad, w_in, w_back,
    norm_src, norm_in, sum_src, sum_in, band_src, band_in,
    send, recv, norm_send, norm_recv, sum_send, sum_recv, band_send, band_recv,
):
    domain = lax.axis_index("space")
    image = lax.axis_index("image")
    upper = lax.rem(domain + 1, n_space)
    lower = lax.rem(domain + n_space - 1, n_space)
    following = lax.rem(image + 1, n_image)
    previous = lax.rem(image + n_image - 1, n_image)
    per_atom, atoms = nb_t.shape
    ext = 3 * atoms
    chunks, pairs = oh.shape[0], oh.shape[1]
    basis = fin_ref.shape[1]
    channels = emb_ref.shape[1]

    sources = (
        pos_hbm, vel_hbm, emb_hbm, nb_hbm, up_hbm, down_hbm, climb_hbm, reset_hbm,
        fin_hbm, fout_hbm, uw_hbm, read_hbm, spring_hbm, step_hbm, mix_hbm,
    )
    targets = (
        pos_ref, vel_ref, emb_ref, nb_t, up_ref, down_ref, climb_ref, reset_ref,
        fin_ref, fout_ref, uw_ref, read_ref, spring_ref, step_ref, mix_ref,
    )
    fetches = [
        pltpu.make_async_copy(source, target, fetch_sem.at[i])
        for i, (source, target) in enumerate(zip(sources, targets))
    ]
    for i in (0, 4, 5, 2, 3, 8, 9, 10, 1, 11, 6, 7, 12, 13, 14):
        fetches[i].start()

    barrier = pltpu.get_barrier_semaphore()
    for i in range(1, n_space):
        pl.semaphore_signal(
            barrier, inc=1, device_id={"space": lax.rem(domain + i, n_space)}, device_id_type=MESH
        )
    for i in range(1, n_image):
        pl.semaphore_signal(
            barrier, inc=1, device_id={"image": lax.rem(image + i, n_image)}, device_id_type=MESH
        )

    def remote(src, dst, slot, where):
        return pltpu.make_async_remote_copy(
            src_ref=src, dst_ref=dst, send_sem=send.at[slot], recv_sem=recv.at[slot],
            device_id=where, device_id_type=MESH,
        )

    def spread(src, dst, out_sem, in_sem, axis, me, count):
        copies = []
        for i in range(1, count):
            copies.append(
                pltpu.make_async_remote_copy(
                    src_ref=src, dst_ref=dst.at[me], send_sem=out_sem.at[i], recv_sem=in_sem.at[me],
                    device_id={axis: lax.rem(me + i, count)}, device_id_type=MESH,
                )
            )
        for copy in copies:
            copy.start()
        dst[me] = src[...]

        def finish():
            for i in range(1, count):
                other = lax.rem(me + i, count)
                pltpu.make_async_remote_copy(
                    src_ref=src, dst_ref=dst.at[other], send_sem=out_sem.at[i],
                    recv_sem=in_sem.at[other], device_id={axis: other}, device_id_type=MESH,
                ).wait_recv()
            for copy in copies:
                copy.wait_send()

        return finish

    for i in (0, 4, 5, 2):
        fetches[i].wait()
    pos8[...] = jnp.zeros_like(pos8)
    for r in range(3):
        pos8[r : r + 1, :] = pos_ref[r]
    here = pos8[...]
    part_a = here.astype(BF16).astype(F32)
    rest = here - part_a
    part_b = rest.astype(BF16).astype(F32)
    part_c = rest - part_b
    parts = jnp.concatenate([part_a, part_b, part_c, jnp.zeros_like(here)], axis=0).astype(BF16)
    coord[0] = parts
    atom_rows = lax.broadcasted_iota(jnp.int32, (atoms, atoms), 0)
    embed = emb_ref[...]
    ext_emb[0:atoms, :] = embed
    for side, ids in ((0, up_ref), (1, down_ref)):
        picked = jnp.where(atom_rows == ids[...], 1.0, 0.0)
        sel_t[side] = picked.astype(BF16)
        sel[side] = picked.T.astype(BF16)
        coord_src[side] = dot(parts, sel_t[side]).astype(BF16)
        emb_src[side] = dot(sel[side], embed).astype(BF16)

    pl.semaphore_wait(barrier, n_space + n_image - 2)
    to_up, to_down = {"space": upper}, {"space": lower}
    coord_copies = [
        remote(coord_src.at[0], coord.at[1], 0, to_up),
        remote(coord_src.at[1], coord.at[2], 1, to_down),
    ]
    emb_copies = [
        remote(emb_src.at[0], ext_emb.at[pl.ds(atoms, atoms)], 2, to_up),
        remote(emb_src.at[1], ext_emb.at[pl.ds(2 * atoms, atoms)], 3, to_down),
    ]
    image_copies = [
        remote(pos8, prev8, 4, {"image": following}),
        remote(pos8, next8, 5, {"image": previous}),
    ]
    for copy in coord_copies + emb_copies + image_copies:
        copy.start()

    for i in (3, 8, 9, 10, 1, 11, 6, 7, 12, 13, 14):
        fetches[i].wait()
    nb = nb_t[...].T
    per_chunk = pairs // atoms
    ext_lane = lax.broadcasted_iota(jnp.int32, (atoms, ext), 1)
    for k in range(per_atom):
        c, r = k // per_chunk, k % per_chunk
        oh[c, r * atoms : (r + 1) * atoms, :] = onehot(nb[:, k : k + 1] == ext_lane)
    ext_row = lax.broadcasted_iota(jnp.int32, (ext, pairs), 0)
    def slot_row(c):
        return jnp.concatenate(
            [nb_t[pl.ds(c * per_chunk + r, 1), :] for r in range(per_chunk)], axis=1
        )

    def build(c, carry):
        oht[c] = onehot(slot_row(c) == ext_row)
        return carry

    lax.fori_loop(0, chunks, build, 0, unroll=1)
    for layer in range(2):
        high, low = split_two(fin_ref[layer])
        lanes = slice(layer * channels, (layer + 1) * channels)
        w_in[:, lanes] = jnp.concatenate([high, high, low], axis=0)
        w_back[layer] = jnp.concatenate([high, low], axis=0)

    for copy in coord_copies + emb_copies:
        copy.wait_recv()

    low_shift = jnp.where(domain == 0, -n_space, 0).astype(F32)
    high_shift = jnp.where(domain == n_space - 1, n_space, 0).astype(F32)
    all_coord = jnp.concatenate([coord[0], coord[1], coord[2]], axis=1)
    here_wide = jnp.concatenate([here] * per_chunk, axis=1)
    first_row = lax.broadcasted_iota(jnp.int32, (8, pairs), 0) == 0
    centres = lax.broadcasted_iota(jnp.int32, (basis, pairs), 0).astype(F32) * (
        BASIS_REACH / (basis - 1)
    )
    ext_embed = ext_emb[...]
    fout_one, fout_two = fout_ref[0], fout_ref[1]

    def fold(values):
        total = values[0:atoms]
        for r in range(1, per_chunk):
            total = total + values[r * atoms : (r + 1) * atoms]
        return total

    def repeat(values):
        return jnp.concatenate([values] * per_chunk, axis=0)

    def layer_one(c, total):
        found = dot(all_coord, oht[c])
        slots = slot_row(c)
        shift = jnp.where(
            slots >= 2 * atoms, high_shift, jnp.where(slots >= atoms, low_shift, 0.0)
        )
        there = found[0:8] + found[8:16] + found[16:24]
        vec = there + jnp.where(first_row, shift, 0.0) - here_wide
        pv_all[c] = vec
        sq_dist = jnp.sum(vec * vec, axis=0, keepdims=True)
        scaled = (sq_dist - centres) * (1.0 / BASIS_WIDTH)
        radial = jnp.exp(-scaled * scaled)
        slope_all[c] = radial * (-2.0 / BASIS_WIDTH) * scaled
        high, low = split_two(radial)
        pre = dot_tn(jnp.concatenate([high, low, high], axis=0), w_in[...])
        pre_two[c] = pre[:, channels:]
        pre_one = pre[:, :channels]
        sig = gate(pre_one)
        act = pre_one * sig
        sig, act = sig.astype(BF16), act.astype(BF16)
        ds_one[c] = sig + act * (1.0 - sig)
        filt = dot(act, fout_one)
        rows = dot(oh[c], ext_embed)
        rows_one[c] = rows.astype(BF16)
        return total + fold(filt * rows)

    zeros = jnp.zeros((atoms, channels), F32)
    msg_one = lax.fori_loop(0, chunks, layer_one, zeros, unroll=2)
    upd_one = dot(msg_one.astype(BF16), uw_ref[0])
    sig_one = gate(upd_one)
    act_one = upd_one * sig_one
    slope_one = sig_one + act_one * (1.0 - sig_one)
    hidden = (embed.astype(F32) + act_one).astype(BF16)
    ext_hid[0:atoms, :] = hidden
    hid_src[0] = dot(sel[0], hidden).astype(BF16)
    hid_src[1] = dot(sel[1], hidden).astype(BF16)
    hid_copies = [
        remote(hid_src.at[0], ext_hid.at[pl.ds(atoms, atoms)], 6, to_up),
        remote(hid_src.at[1], ext_hid.at[pl.ds(2 * atoms, atoms)], 7, to_down),
    ]
    for copy in hid_copies:
        copy.start()

    for copy in image_copies:
        copy.wait_recv()
    ahead = jnp.where(image == n_image - 1, 0.0, next8[...]) - here
    behind = here - jnp.where(image == 0, 0.0, prev8[...])
    row8 = lax.broadcasted_iota(jnp.int32, (8, atoms), 0)

    def place(values):
        block = jnp.zeros((8, atoms), F32)
        for r, value in enumerate(values):
            block = jnp.where(row8 == r, value, block)
        return block

    def rows_sum(values):
        return jnp.sum(values, axis=0, keepdims=True)

    norm_src[...] = place([rows_sum(ahead * ahead), rows_sum(behind * behind)])
    norm_done = spread(norm_src, norm_in, norm_send, norm_recv, "space", domain, n_space)

    def filter_two(c, carry):
        pre = pre_two[c]
        sig = gate(pre)
        act = pre * sig
        sig, act = sig.astype(BF16), act.astype(BF16)
        ds_two[c] = sig + act * (1.0 - sig)
        filt_two[c] = dot(act, fout_two)
        return carry

    lax.fori_loop(0, chunks, filter_two, 0, unroll=4)
    for copy in hid_copies:
        copy.wait_recv()
    ext_hidden = ext_hid[...]

    def layer_two(c, total):
        rows = dot(oh[c], ext_hidden)
        rows_two[c] = rows.astype(BF16)
        return total + fold(filt_two[c] * rows)

    msg_two = lax.fori_loop(0, chunks, layer_two, zeros, unroll=4)
    upd_two = dot(msg_two.astype(BF16), uw_ref[1])
    sig_two = gate(upd_two)
    act_two = upd_two * sig_two
    readout = read_ref[...]
    energy_row = rows_sum(act_two * readout)
    dupd_two = ((sig_two + act_two * (1.0 - sig_two)) * readout).astype(BF16)
    dmsg_two = dot_nt(dupd_two, uw_ref[1])

    grad_all[...] = jnp.zeros_like(grad_all)
    group = 2

    def scatter_two(g, carry):
        picks, sources = [], []
        for i in range(group):
            c = g * group + i
            picks.append(oht[c])
            sources.append((filt_two[c] * repeat(dmsg_two)).astype(BF16))
        grad_all[...] += dot(
            jnp.concatenate(picks, axis=1), jnp.concatenate(sources, axis=0)
        )
        return carry

    lax.fori_loop(0, chunks // group, scatter_two, 0)
    grad_src[0] = grad_all[atoms : 2 * atoms, :].astype(BF16)
    grad_src[1] = grad_all[2 * atoms : 3 * atoms, :].astype(BF16)
    grad_copies = [
        remote(grad_src.at[0], grad_in.at[0], 8, to_down),
        remote(grad_src.at[1], grad_in.at[1], 9, to_up),
    ]
    for copy in grad_copies:
        copy.start()

    def back(dmsg, rows, weight, slope, layer):
        dact = dot_nt(repeat(dmsg) * rows, weight)
        dpre = dact.astype(BF16) * slope
        both = dot_nt(w_back[layer], dpre)
        return both[:basis] + both[basis:]

    def back_two(c, carry):
        drad[c] = back(dmsg_two_low, rows_two[c], fout_two, ds_two[c], 1)
        return carry

    dmsg_two_low = dmsg_two.astype(BF16)
    lax.fori_loop(0, chunks, back_two, 0, unroll=4)
    for copy in grad_copies:
        copy.wait_recv()
    dhidden = grad_all[0:atoms, :] + dot(sel_t[0], grad_in[0]) + dot(sel_t[1], grad_in[1])
    dupd_one = (dhidden * slope_one).astype(BF16)
    dmsg_one = dot_nt(dupd_one, uw_ref[0]).astype(BF16)

    def back_one(c, carry):
        own, scattered = carry
        dradial = drad[c] + back(dmsg_one, rows_one[c], fout_one, ds_one[c], 0)
        dsq = jnp.sum(dradial * slope_all[c], axis=0, keepdims=True)
        pair = (2.0 * dsq) * pv_all[c]
        for r in range(per_chunk):
            own = own + pair[:, r * atoms : (r + 1) * atoms]
        high = pair.astype(BF16).astype(F32)
        both = jnp.concatenate([high, pair - high], axis=0).astype(BF16)
        return own, scattered + dot(both, oh[c])

    own, scattered = lax.fori_loop(
        0, chunks, back_one, (jnp.zeros((8, atoms), F32), jnp.zeros((16, ext), F32)),
        unroll=2,
    )
    scattered = scattered[0:8] + scattered[8:16]
    force_src[0] = scattered[:, atoms : 2 * atoms]
    force_src[1] = scattered[:, 2 * atoms : 3 * atoms]
    force_copies = [
        remote(force_src.at[0], force_in.at[0], 10, to_down),
        remote(force_src.at[1], force_in.at[1], 11, to_up),
    ]
    for copy in force_copies:
        copy.start()

    norm_done()
    norm_sum = norm_in[0]
    for i in range(1, n_space):
        norm_sum = norm_sum + norm_in[i]
    norms = jnp.sqrt(jnp.sum(norm_sum, axis=1, keepdims=True) + EPSILON)
    ahead_norm, behind_norm = norms[0:1], norms[1:2]
    tangent = ahead / ahead_norm + behind / behind_norm
    tangent_row = rows_sum(tangent * tangent)
    speed = place([vel_ref[r] for r in range(3)])
    speed_row = rows_sum(speed * speed)
    spring_part = spring_ref[...] * (ahead_norm - behind_norm)
    local_force = own - scattered[:, 0:atoms]
    for copy in force_copies:
        copy.wait_recv()

    def returned(side):
        ghost = force_in[side]
        high = ghost.astype(BF16).astype(F32)
        both = dot(jnp.concatenate([high, ghost - high], axis=0).astype(BF16), sel[side])
        return both[0:8] + both[8:16]

    forces = local_force - returned(0) - returned(1)
    sum_src[...] = place(
        [
            rows_sum(forces * forces), rows_sum(forces * tangent), tangent_row, energy_row,
            speed_row,
        ]
    )
    sum_done = spread(sum_src, sum_in, sum_send, sum_recv, "space", domain, n_space)
    sum_done()
    sums = sum_in[0]
    for i in range(1, n_space):
        sums = sums + sum_in[i]
    sums = jnp.sum(sums, axis=1, keepdims=True)
    force_sq, along, tangent_sq = sums[0:1], sums[1:2], sums[2:3]
    energy_ref[...] = sums[3:4]
    scale = 1.0 / jnp.sqrt(tangent_sq + EPSILON)
    parallel = along * scale
    unit_sq = tangent_sq * scale * scale
    climbing = climb_ref[...] > 0
    take = jnp.where(climbing, 2.0 * parallel, parallel - spring_part)
    movable = jnp.where((image > 0) & (image < n_image - 1), 1.0, 0.0)
    band_sq = jnp.maximum(force_sq - 2.0 * take * parallel + take * take * unit_sq, 0.0)
    band_src[...] = place([band_sq * movable, sums[4:5] * movable])
    band_done = spread(band_src, band_in, band_send, band_recv, "image", image, n_image)
    band_force = (forces - take * (tangent * scale)) * movable
    band_done()
    totals = band_in[0]
    for i in range(1, n_image):
        totals = totals + band_in[i]
    totals = jnp.sqrt(totals + EPSILON)
    force_norm, speed_norm = totals[0:1], totals[1:2]
    mixing = mix_ref[...]
    time_step = step_ref[...]
    mixed = (1.0 - mixing) * speed + mixing * (speed_norm / force_norm) * band_force
    kept = jnp.where(reset_ref[...] > 0, 0.0, mixed)
    new_speed = (kept + time_step * band_force) * movable
    new_place = here + time_step * new_speed
    for r in range(3):
        newvel_ref[r] = new_speed[r : r + 1]
        newpos_ref[r] = new_place[r : r + 1]
    for copy in (
        coord_copies + emb_copies + image_copies + hid_copies + grad_copies + force_copies
    ):
        copy.wait_send()


def per_device(
    n_space, n_image,
    positions, velocity, embed, neighbours, send_up, send_down, climb, reset,
    filter_in, filter_out, update_weight, readout, spring, time_step, mixing,
):
    atoms, per_atom = neighbours.shape
    channels = embed.shape[1]
    basis = filter_in.shape[1]
    per_chunk = 4
    chunks, pairs = per_atom // per_chunk, per_chunk * atoms
    ext = 3 * atoms
    vmem = pl.BlockSpec(memory_space=pltpu.VMEM)
    hbm = pl.BlockSpec(memory_space=pltpu.HBM)
    dma = pltpu.SemaphoreType.DMA
    basis_shape = filter_in.shape
    scratch = [
        pltpu.VMEM((3, 1, atoms), F32),
        pltpu.VMEM((3, 1, atoms), F32),
        pltpu.VMEM((atoms, channels), BF16),
        pltpu.VMEM((per_atom, atoms), jnp.int32),
        pltpu.VMEM((1, atoms), jnp.int32),
        pltpu.VMEM((1, atoms), jnp.int32),
        pltpu.VMEM((1, 1), jnp.int32),
        pltpu.VMEM((1, 1), jnp.int32),
        pltpu.VMEM(basis_shape, F32),
        pltpu.VMEM((2, channels, channels), BF16),
        pltpu.VMEM((2, channels, channels), BF16),
        pltpu.VMEM((1, channels), F32),
        pltpu.VMEM((1, 1), F32),
        pltpu.VMEM((1, 1), F32),
        pltpu.VMEM((1, 1), F32),
        dma((15,)),
        pltpu.VMEM((8, atoms), F32),
        pltpu.VMEM((8, atoms), F32),
        pltpu.VMEM((8, atoms), F32),
        pltpu.VMEM((3, 32, atoms), BF16),
        pltpu.VMEM((2, 32, atoms), BF16),
        pltpu.VMEM((ext, channels), BF16),
        pltpu.VMEM((2, atoms, channels), BF16),
        pltpu.VMEM((ext, channels), BF16),
        pltpu.VMEM((2, atoms, channels), BF16),
        pltpu.VMEM((ext, channels), F32),
        pltpu.VMEM((2, atoms, channels), BF16),
        pltpu.VMEM((2, atoms, channels), BF16),
        pltpu.VMEM((2, 8, atoms), F32),
        pltpu.VMEM((2, 8, atoms), F32),
        pltpu.VMEM((2, atoms, atoms), BF16),
        pltpu.VMEM((2, atoms, atoms), BF16),
        pltpu.VMEM((chunks, pairs, ext), BF16),
        pltpu.VMEM((chunks, ext, pairs), BF16),
        pltpu.VMEM((chunks, 8, pairs), F32),
        pltpu.VMEM((chunks, basis, pairs), F32),
        pltpu.VMEM((chunks, pairs, channels), F32),
        pltpu.VMEM((chunks, pairs, channels), BF16),
        pltpu.VMEM((chunks, pairs, channels), BF16),
        pltpu.VMEM((chunks, pairs, channels), BF16),
        pltpu.VMEM((chunks, pairs, channels), BF16),
        pltpu.VMEM((chunks, pairs, channels), F32),
        pltpu.VMEM((chunks, basis, pairs), F32),
        pltpu.VMEM((3 * basis, 2 * channels), BF16),
        pltpu.VMEM((2, 2 * basis, channels), BF16),
        pltpu.VMEM((8, atoms), F32),
        pltpu.VMEM((n_space, 8, atoms), F32),
        pltpu.VMEM((8, atoms), F32),
        pltpu.VMEM((n_space, 8, atoms), F32),
        pltpu.VMEM((8, atoms), F32),
        pltpu.VMEM((n_image, 8, atoms), F32),
        dma((12,)), dma((12,)),
        dma((n_space,)), dma((n_space,)),
        dma((n_space,)), dma((n_space,)),
        dma((n_image,)), dma((n_image,)),
    ]
    new_pos, new_vel, energy = pl.pallas_call(
        functools.partial(body, n_space, n_image),
        out_shape=(
            jax.ShapeDtypeStruct((3, 1, atoms), F32),
            jax.ShapeDtypeStruct((3, 1, atoms), F32),
            jax.ShapeDtypeStruct((1, 1), F32),
        ),
        in_specs=[hbm] * 15,
        out_specs=(vmem, vmem, vmem),
        scratch_shapes=scratch,
        compiler_params=pltpu.CompilerParams(
            collective_id=0, has_side_effects=True, vmem_limit_bytes=60 * 1024 * 1024
        ),
    )(
        jnp.transpose(positions, (1, 0, 2)), jnp.transpose(velocity, (1, 0, 2)), embed,
        neighbours.T, send_up.reshape(1, -1), send_down.reshape(1, -1), climb.reshape(1, 1), reset.reshape(1, 1),
        filter_in, filter_out, update_weight, readout.reshape(1, -1),
        spring.reshape(1, 1), time_step.reshape(1, 1), mixing.reshape(1, 1),
    )
    back = (1, 0, 2)
    return jnp.transpose(new_pos, back), jnp.transpose(new_vel, back), energy.reshape(1)


def solution(mesh):
    placed = (
        P("image", None, "space"), P("image", None, "space"), P("space", None), P("space", None),
        P("space"), P("space"), P("image"), P("image"), P(), P(), P(), P(), P(), P(), P(),
    )
    return jax.shard_map(
        functools.partial(per_device, mesh.shape["space"], mesh.shape["image"]),
        mesh=mesh,
        in_specs=placed,
        out_specs=(P("image", None, "space"), P("image", None, "space"), P("image")),
        check_vma=False,
    )
```

```python
import functools
import jax
import jax.numpy as jnp
from jax import lax
from jax.experimental import pallas as pl
from jax.experimental.pallas import tpu as pltpu
from jax.sharding import PartitionSpec as P

EPSILON = 1e-06
BASIS_WIDTH = 0.6
BASIS_REACH = 6.0
F32 = jnp.float32
BF16 = jnp.bfloat16
MESH = pl.DeviceIdType.MESH


def dot(left, right):
    return jnp.dot(left, right, preferred_element_type=F32)


def dot_nt(left, right):
    return lax.dot_general(left, right, (((1,), (1,)), ((), ())), preferred_element_type=F32)


def dot_tn(left, right):
    return lax.dot_general(left, right, (((0,), (0,)), ((), ())), preferred_element_type=F32)


def gate(values):
    return 0.5 * jnp.tanh(0.5 * values) + 0.5


def split_two(values):
    high = values.astype(BF16)
    low = (values - high.astype(F32)).astype(BF16)
    return high, low


def onehot(mask):
    return jnp.where(mask, 1.0, 0.0).astype(BF16)


def body(
    n_space, n_image,
    pos_hbm, vel_hbm, emb_hbm, nb_hbm, up_hbm, down_hbm, climb_hbm, reset_hbm,
    fin_hbm, fout_hbm, uw_hbm, read_hbm, spring_hbm, step_hbm, mix_hbm,
    newpos_ref, newvel_ref, energy_ref,
    pos_ref, vel_ref, emb_ref, nb_t, up_ref, down_ref, climb_ref, reset_ref,
    fin_ref, fout_ref, uw_ref, read_ref, spring_ref, step_ref, mix_ref, fetch_sem,
    pos8, prev8, next8, coord, coord_src, ext_emb, emb_src, ext_hid, hid_src,
    grad_all, grad_src, grad_in, force_src, force_in,
    sel, sel_t, oh, oht, pv_all, slope_all, pre_two, ds_one, ds_two,
    rows_one, rows_two, filt_two, drad, w_in, w_back,
    norm_src, norm_in, sum_src, sum_in, band_src, band_in,
    send, recv, norm_send, norm_recv, sum_send, sum_recv, band_send, band_recv,
):
    domain = lax.axis_index("space")
    image = lax.axis_index("image")
    upper = lax.rem(domain + 1, n_space)
    lower = lax.rem(domain + n_space - 1, n_space)
    following = lax.rem(image + 1, n_image)
    previous = lax.rem(image + n_image - 1, n_image)
    per_atom, atoms = nb_t.shape
    ext = 3 * atoms
    chunks, pairs = oh.shape[0], oh.shape[1]
    basis = fin_ref.shape[1]
    channels = emb_ref.shape[1]

    sources = (
        pos_hbm, vel_hbm, emb_hbm, nb_hbm, up_hbm, down_hbm, climb_hbm, reset_hbm,
        fin_hbm, fout_hbm, uw_hbm, read_hbm, spring_hbm, step_hbm, mix_hbm,
    )
    targets = (
        pos_ref, vel_ref, emb_ref, nb_t, up_ref, down_ref, climb_ref, reset_ref,
        fin_ref, fout_ref, uw_ref, read_ref, spring_ref, step_ref, mix_ref,
    )
    fetches = [
        pltpu.make_async_copy(source, target, fetch_sem.at[i])
        for i, (source, target) in enumerate(zip(sources, targets))
    ]
    for i in (0, 4, 5, 2, 3, 8, 9, 10, 1, 11, 6, 7, 12, 13, 14):
        fetches[i].start()

    barrier = pltpu.get_barrier_semaphore()
    for i in range(1, n_space):
        pl.semaphore_signal(
            barrier, inc=1, device_id={"space": lax.rem(domain + i, n_space)}, device_id_type=MESH
        )
    for i in range(1, n_image):
        pl.semaphore_signal(
            barrier, inc=1, device_id={"image": lax.rem(image + i, n_image)}, device_id_type=MESH
        )

    def remote(src, dst, slot, where):
        return pltpu.make_async_remote_copy(
            src_ref=src, dst_ref=dst, send_sem=send.at[slot], recv_sem=recv.at[slot],
            device_id=where, device_id_type=MESH,
        )

    def spread(src, dst, out_sem, in_sem, axis, me, count):
        copies = []
        for i in range(1, count):
            copies.append(
                pltpu.make_async_remote_copy(
                    src_ref=src, dst_ref=dst.at[me], send_sem=out_sem.at[i], recv_sem=in_sem.at[me],
                    device_id={axis: lax.rem(me + i, count)}, device_id_type=MESH,
                )
            )
        for copy in copies:
            copy.start()
        dst[me] = src[...]

        def finish():
            for i in range(1, count):
                other = lax.rem(me + i, count)
                pltpu.make_async_remote_copy(
                    src_ref=src, dst_ref=dst.at[other], send_sem=out_sem.at[i],
                    recv_sem=in_sem.at[other], device_id={axis: other}, device_id_type=MESH,
                ).wait_recv()
            for copy in copies:
                copy.wait_send()

        return finish

    for i in (0, 4, 5, 2):
        fetches[i].wait()
    pos8[...] = jnp.zeros_like(pos8)
    for r in range(3):
        pos8[r : r + 1, :] = pos_ref[r]
    here = pos8[...]
    part_a = here.astype(BF16).astype(F32)
    rest = here - part_a
    part_b = rest.astype(BF16).astype(F32)
    part_c = rest - part_b
    parts = jnp.concatenate([part_a, part_b, part_c, jnp.zeros_like(here)], axis=0).astype(BF16)
    coord[0] = parts
    atom_rows = lax.broadcasted_iota(jnp.int32, (atoms, atoms), 0)
    embed = emb_ref[...]
    ext_emb[0:atoms, :] = embed
    for side, ids in ((0, up_ref), (1, down_ref)):
        picked = jnp.where(atom_rows == ids[...], 1.0, 0.0)
        sel_t[side] = picked.astype(BF16)
        sel[side] = picked.T.astype(BF16)
        coord_src[side] = dot(parts, sel_t[side]).astype(BF16)
        emb_src[side] = dot(sel[side], embed).astype(BF16)

    pl.semaphore_wait(barrier, n_space + n_image - 2)
    to_up, to_down = {"space": upper}, {"space": lower}
    coord_copies = [
        remote(coord_src.at[0], coord.at[1], 0, to_up),
        remote(coord_src.at[1], coord.at[2], 1, to_down),
    ]
    emb_copies = [
        remote(emb_src.at[0], ext_emb.at[pl.ds(atoms, atoms)], 2, to_up),
        remote(emb_src.at[1], ext_emb.at[pl.ds(2 * atoms, atoms)], 3, to_down),
    ]
    image_copies = [
        remote(pos8, prev8, 4, {"image": following}),
        remote(pos8, next8, 5, {"image": previous}),
    ]
    for copy in coord_copies + emb_copies + image_copies:
        copy.start()

    for i in (3, 8, 9, 10, 1, 11, 6, 7, 12, 13, 14):
        fetches[i].wait()
    nb = nb_t[...].T
    per_chunk = pairs // atoms
    ext_lane = lax.broadcasted_iota(jnp.int32, (atoms, ext), 1)
    for k in range(per_atom):
        c, r = k // per_chunk, k % per_chunk
        oh[c, r * atoms : (r + 1) * atoms, :] = onehot(nb[:, k : k + 1] == ext_lane)
    ext_row = lax.broadcasted_iota(jnp.int32, (ext, pairs), 0)
    def slot_row(c):
        return jnp.concatenate(
            [nb_t[pl.ds(c * per_chunk + r, 1), :] for r in range(per_chunk)], axis=1
        )

    def build(c, carry):
        oht[c] = onehot(slot_row(c) == ext_row)
        return carry

    lax.fori_loop(0, chunks, build, 0, unroll=1)
    for layer in range(2):
        high, low = split_two(fin_ref[layer])
        lanes = slice(layer * channels, (layer + 1) * channels)
        w_in[:, lanes] = jnp.concatenate([high, high, low], axis=0)
        w_back[layer] = jnp.concatenate([high, low], axis=0)

    for copy in coord_copies + emb_copies:
        copy.wait_recv()

    low_shift = jnp.where(domain == 0, -n_space, 0).astype(F32)
    high_shift = jnp.where(domain == n_space - 1, n_space, 0).astype(F32)
    all_coord = jnp.concatenate([coord[0], coord[1], coord[2]], axis=1)
    here_wide = jnp.concatenate([here] * per_chunk, axis=1)
    first_row = lax.broadcasted_iota(jnp.int32, (8, pairs), 0) == 0
    centres = lax.broadcasted_iota(jnp.int32, (basis, pairs), 0).astype(F32) * (
        BASIS_REACH / (basis - 1)
    )
    ext_embed = ext_emb[...]
    fout_one, fout_two = fout_ref[0], fout_ref[1]

    def fold(values):
        total = values[0:atoms]
        for r in range(1, per_chunk):
            total = total + values[r * atoms : (r + 1) * atoms]
        return total

    def repeat(values):
        return jnp.concatenate([values] * per_chunk, axis=0)

    def layer_one(c, total):
        found = dot(all_coord, oht[c])
        slots = slot_row(c)
        shift = jnp.where(
            slots >= 2 * atoms, high_shift, jnp.where(slots >= atoms, low_shift, 0.0)
        )
        there = found[0:8] + found[8:16] + found[16:24]
        vec = there + jnp.where(first_row, shift, 0.0) - here_wide
        pv_all[c] = vec
        sq_dist = jnp.sum(vec * vec, axis=0, keepdims=True)
        scaled = (sq_dist - centres) * (1.0 / BASIS_WIDTH)
        radial = jnp.exp(-scaled * scaled)
        slope_all[c] = radial * (-2.0 / BASIS_WIDTH) * scaled
        high, low = split_two(radial)
        pre = dot_tn(jnp.concatenate([high, low, high], axis=0), w_in[...])
        pre_two[c] = pre[:, channels:]
        pre_one = pre[:, :channels]
        sig = gate(pre_one)
        act = pre_one * sig
        sig, act = sig.astype(BF16), act.astype(BF16)
        ds_one[c] = sig + act * (1.0 - sig)
        filt = dot(act, fout_one)
        rows = dot(oh[c], ext_embed)
        rows_one[c] = rows.astype(BF16)
        return total + fold(filt * rows)

    zeros = jnp.zeros((atoms, channels), F32)
    msg_one = lax.fori_loop(0, chunks, layer_one, zeros, unroll=2)
    upd_one = dot(msg_one.astype(BF16), uw_ref[0])
    sig_one = gate(upd_one)
    act_one = upd_one * sig_one
    slope_one = sig_one + act_one * (1.0 - sig_one)
    hidden = (embed.astype(F32) + act_one).astype(BF16)
    ext_hid[0:atoms, :] = hidden
    hid_src[0] = dot(sel[0], hidden).astype(BF16)
    hid_src[1] = dot(sel[1], hidden).astype(BF16)
    hid_copies = [
        remote(hid_src.at[0], ext_hid.at[pl.ds(atoms, atoms)], 6, to_up),
        remote(hid_src.at[1], ext_hid.at[pl.ds(2 * atoms, atoms)], 7, to_down),
    ]
    for copy in hid_copies:
        copy.start()

    for copy in image_copies:
        copy.wait_recv()
    ahead = jnp.where(image == n_image - 1, 0.0, next8[...]) - here
    behind = here - jnp.where(image == 0, 0.0, prev8[...])
    row8 = lax.broadcasted_iota(jnp.int32, (8, atoms), 0)

    def place(values):
        block = jnp.zeros((8, atoms), F32)
        for r, value in enumerate(values):
            block = jnp.where(row8 == r, value, block)
        return block

    def rows_sum(values):
        return jnp.sum(values, axis=0, keepdims=True)

    norm_src[...] = place([rows_sum(ahead * ahead), rows_sum(behind * behind)])
    norm_done = spread(norm_src, norm_in, norm_send, norm_recv, "space", domain, n_space)

    def filter_two(c, carry):
        pre = pre_two[c]
        sig = gate(pre)
        act = pre * sig
        sig, act = sig.astype(BF16), act.astype(BF16)
        ds_two[c] = sig + act * (1.0 - sig)
        filt_two[c] = dot(act, fout_two)
        return carry

    lax.fori_loop(0, chunks, filter_two, 0, unroll=2)
    for copy in hid_copies:
        copy.wait_recv()
    ext_hidden = ext_hid[...]

    def layer_two(c, total):
        rows = dot(oh[c], ext_hidden)
        rows_two[c] = rows.astype(BF16)
        return total + fold(filt_two[c] * rows)

    msg_two = lax.fori_loop(0, chunks, layer_two, zeros, unroll=2)
    upd_two = dot(msg_two.astype(BF16), uw_ref[1])
    sig_two = gate(upd_two)
    act_two = upd_two * sig_two
    readout = read_ref[...]
    energy_row = rows_sum(act_two * readout)
    dupd_two = ((sig_two + act_two * (1.0 - sig_two)) * readout).astype(BF16)
    dmsg_two = dot_nt(dupd_two, uw_ref[1])

    grad_all[...] = jnp.zeros_like(grad_all)
    group = 2

    def scatter_two(g, carry):
        picks, sources = [], []
        for i in range(group):
            c = g * group + i
            picks.append(oht[c])
            sources.append((filt_two[c] * repeat(dmsg_two)).astype(BF16))
        grad_all[...] += dot(
            jnp.concatenate(picks, axis=1), jnp.concatenate(sources, axis=0)
        )
        return carry

    lax.fori_loop(0, chunks // group, scatter_two, 0)
    grad_src[0] = grad_all[atoms : 2 * atoms, :].astype(BF16)
    grad_src[1] = grad_all[2 * atoms : 3 * atoms, :].astype(BF16)
    grad_copies = [
        remote(grad_src.at[0], grad_in.at[0], 8, to_down),
        remote(grad_src.at[1], grad_in.at[1], 9, to_up),
    ]
    for copy in grad_copies:
        copy.start()

    def back(dmsg, rows, weight, slope, layer):
        dact = dot_nt(repeat(dmsg) * rows, weight)
        dpre = dact.astype(BF16) * slope
        both = dot_nt(w_back[layer], dpre)
        return both[:basis] + both[basis:]

    def back_two(c, carry):
        drad[c] = back(dmsg_two_low, rows_two[c], fout_two, ds_two[c], 1)
        return carry

    dmsg_two_low = dmsg_two.astype(BF16)
    lax.fori_loop(0, chunks, back_two, 0, unroll=2)
    for copy in grad_copies:
        copy.wait_recv()
    dhidden = grad_all[0:atoms, :] + dot(sel_t[0], grad_in[0]) + dot(sel_t[1], grad_in[1])
    dupd_one = (dhidden * slope_one).astype(BF16)
    dmsg_one = dot_nt(dupd_one, uw_ref[0]).astype(BF16)

    def back_one(c, carry):
        own, scattered = carry
        dradial = drad[c] + back(dmsg_one, rows_one[c], fout_one, ds_one[c], 0)
        dsq = jnp.sum(dradial * slope_all[c], axis=0, keepdims=True)
        pair = (2.0 * dsq) * pv_all[c]
        for r in range(per_chunk):
            own = own + pair[:, r * atoms : (r + 1) * atoms]
        high = pair.astype(BF16).astype(F32)
        both = jnp.concatenate([high, pair - high], axis=0).astype(BF16)
        return own, scattered + dot(both, oh[c])

    own, scattered = lax.fori_loop(
        0, chunks, back_one, (jnp.zeros((8, atoms), F32), jnp.zeros((16, ext), F32)),
        unroll=2,
    )
    scattered = scattered[0:8] + scattered[8:16]
    force_src[0] = scattered[:, atoms : 2 * atoms]
    force_src[1] = scattered[:, 2 * atoms : 3 * atoms]
    force_copies = [
        remote(force_src.at[0], force_in.at[0], 10, to_down),
        remote(force_src.at[1], force_in.at[1], 11, to_up),
    ]
    for copy in force_copies:
        copy.start()

    norm_done()
    norm_sum = norm_in[0]
    for i in range(1, n_space):
        norm_sum = norm_sum + norm_in[i]
    norms = jnp.sqrt(jnp.sum(norm_sum, axis=1, keepdims=True) + EPSILON)
    ahead_norm, behind_norm = norms[0:1], norms[1:2]
    tangent = ahead / ahead_norm + behind / behind_norm
    tangent_row = rows_sum(tangent * tangent)
    speed = place([vel_ref[r] for r in range(3)])
    speed_row = rows_sum(speed * speed)
    spring_part = spring_ref[...] * (ahead_norm - behind_norm)
    local_force = own - scattered[:, 0:atoms]
    for copy in force_copies:
        copy.wait_recv()

    def returned(side):
        ghost = force_in[side]
        high = ghost.astype(BF16).astype(F32)
        both = dot(jnp.concatenate([high, ghost - high], axis=0).astype(BF16), sel[side])
        return both[0:8] + both[8:16]

    forces = local_force - returned(0) - returned(1)
    sum_src[...] = place(
        [
            rows_sum(forces * forces), rows_sum(forces * tangent), tangent_row, energy_row,
            speed_row,
        ]
    )
    sum_done = spread(sum_src, sum_in, sum_send, sum_recv, "space", domain, n_space)
    sum_done()
    sums = sum_in[0]
    for i in range(1, n_space):
        sums = sums + sum_in[i]
    sums = jnp.sum(sums, axis=1, keepdims=True)
    force_sq, along, tangent_sq = sums[0:1], sums[1:2], sums[2:3]
    energy_ref[...] = sums[3:4]
    scale = 1.0 / jnp.sqrt(tangent_sq + EPSILON)
    parallel = along * scale
    unit_sq = tangent_sq * scale * scale
    climbing = climb_ref[...] > 0
    take = jnp.where(climbing, 2.0 * parallel, parallel - spring_part)
    movable = jnp.where((image > 0) & (image < n_image - 1), 1.0, 0.0)
    band_sq = jnp.maximum(force_sq - 2.0 * take * parallel + take * take * unit_sq, 0.0)
    band_src[...] = place([band_sq * movable, sums[4:5] * movable])
    band_done = spread(band_src, band_in, band_send, band_recv, "image", image, n_image)
    band_force = (forces - take * (tangent * scale)) * movable
    band_done()
    totals = band_in[0]
    for i in range(1, n_image):
        totals = totals + band_in[i]
    totals = jnp.sqrt(totals + EPSILON)
    force_norm, speed_norm = totals[0:1], totals[1:2]
    mixing = mix_ref[...]
    time_step = step_ref[...]
    mixed = (1.0 - mixing) * speed + mixing * (speed_norm / force_norm) * band_force
    kept = jnp.where(reset_ref[...] > 0, 0.0, mixed)
    new_speed = (kept + time_step * band_force) * movable
    new_place = here + time_step * new_speed
    for r in range(3):
        newvel_ref[r] = new_speed[r : r + 1]
        newpos_ref[r] = new_place[r : r + 1]
    for copy in (
        coord_copies + emb_copies + image_copies + hid_copies + grad_copies + force_copies
    ):
        copy.wait_send()


def per_device(
    n_space, n_image,
    positions, velocity, embed, neighbours, send_up, send_down, climb, reset,
    filter_in, filter_out, update_weight, readout, spring, time_step, mixing,
):
    atoms, per_atom = neighbours.shape
    channels = embed.shape[1]
    basis = filter_in.shape[1]
    per_chunk = 8
    chunks, pairs = per_atom // per_chunk, per_chunk * atoms
    ext = 3 * atoms
    vmem = pl.BlockSpec(memory_space=pltpu.VMEM)
    hbm = pl.BlockSpec(memory_space=pltpu.HBM)
    dma = pltpu.SemaphoreType.DMA
    basis_shape = filter_in.shape
    scratch = [
        pltpu.VMEM((3, 1, atoms), F32),
        pltpu.VMEM((3, 1, atoms), F32),
        pltpu.VMEM((atoms, channels), BF16),
        pltpu.VMEM((per_atom, atoms), jnp.int32),
        pltpu.VMEM((1, atoms), jnp.int32),
        pltpu.VMEM((1, atoms), jnp.int32),
        pltpu.VMEM((1, 1), jnp.int32),
        pltpu.VMEM((1, 1), jnp.int32),
        pltpu.VMEM(basis_shape, F32),
        pltpu.VMEM((2, channels, channels), BF16),
        pltpu.VMEM((2, channels, channels), BF16),
        pltpu.VMEM((1, channels), F32),
        pltpu.VMEM((1, 1), F32),
        pltpu.VMEM((1, 1), F32),
        pltpu.VMEM((1, 1), F32),
        dma((15,)),
        pltpu.VMEM((8, atoms), F32),
        pltpu.VMEM((8, atoms), F32),
        pltpu.VMEM((8, atoms), F32),
        pltpu.VMEM((3, 32, atoms), BF16),
        pltpu.VMEM((2, 32, atoms), BF16),
        pltpu.VMEM((ext, channels), BF16),
        pltpu.VMEM((2, atoms, channels), BF16),
        pltpu.VMEM((ext, channels), BF16),
        pltpu.VMEM((2, atoms, channels), BF16),
        pltpu.VMEM((ext, channels), F32),
        pltpu.VMEM((2, atoms, channels), BF16),
        pltpu.VMEM((2, atoms, channels), BF16),
        pltpu.VMEM((2, 8, atoms), F32),
        pltpu.VMEM((2, 8, atoms), F32),
        pltpu.VMEM((2, atoms, atoms), BF16),
        pltpu.VMEM((2, atoms, atoms), BF16),
        pltpu.VMEM((chunks, pairs, ext), BF16),
        pltpu.VMEM((chunks, ext, pairs), BF16),
        pltpu.VMEM((chunks, 8, pairs), F32),
        pltpu.VMEM((chunks, basis, pairs), F32),
        pltpu.VMEM((chunks, pairs, channels), F32),
        pltpu.VMEM((chunks, pairs, channels), BF16),
        pltpu.VMEM((chunks, pairs, channels), BF16),
        pltpu.VMEM((chunks, pairs, channels), BF16),
        pltpu.VMEM((chunks, pairs, channels), BF16),
        pltpu.VMEM((chunks, pairs, channels), F32),
        pltpu.VMEM((chunks, basis, pairs), F32),
        pltpu.VMEM((3 * basis, 2 * channels), BF16),
        pltpu.VMEM((2, 2 * basis, channels), BF16),
        pltpu.VMEM((8, atoms), F32),
        pltpu.VMEM((n_space, 8, atoms), F32),
        pltpu.VMEM((8, atoms), F32),
        pltpu.VMEM((n_space, 8, atoms), F32),
        pltpu.VMEM((8, atoms), F32),
        pltpu.VMEM((n_image, 8, atoms), F32),
        dma((12,)), dma((12,)),
        dma((n_space,)), dma((n_space,)),
        dma((n_space,)), dma((n_space,)),
        dma((n_image,)), dma((n_image,)),
    ]
    new_pos, new_vel, energy = pl.pallas_call(
        functools.partial(body, n_space, n_image),
        out_shape=(
            jax.ShapeDtypeStruct((3, 1, atoms), F32),
            jax.ShapeDtypeStruct((3, 1, atoms), F32),
            jax.ShapeDtypeStruct((1, 1), F32),
        ),
        in_specs=[hbm] * 15,
        out_specs=(vmem, vmem, vmem),
        scratch_shapes=scratch,
        compiler_params=pltpu.CompilerParams(
            collective_id=0, has_side_effects=True, vmem_limit_bytes=60 * 1024 * 1024
        ),
    )(
        jnp.transpose(positions, (1, 0, 2)), jnp.transpose(velocity, (1, 0, 2)), embed,
        neighbours.T, send_up.reshape(1, -1), send_down.reshape(1, -1), climb.reshape(1, 1), reset.reshape(1, 1),
        filter_in, filter_out, update_weight, readout.reshape(1, -1),
        spring.reshape(1, 1), time_step.reshape(1, 1), mixing.reshape(1, 1),
    )
    back = (1, 0, 2)
    return jnp.transpose(new_pos, back), jnp.transpose(new_vel, back), energy.reshape(1)


def solution(mesh):
    placed = (
        P("image", None, "space"), P("image", None, "space"), P("space", None), P("space", None),
        P("space"), P("space"), P("image"), P("image"), P(), P(), P(), P(), P(), P(), P(),
    )
    return jax.shard_map(
        functools.partial(per_device, mesh.shape["space"], mesh.shape["image"]),
        mesh=mesh,
        in_specs=placed,
        out_specs=(P("image", None, "space"), P("image", None, "space"), P("image")),
        check_vma=False,
    )
```

```python
import functools
import jax
import jax.numpy as jnp
from jax import lax
from jax.experimental import pallas as pl
from jax.experimental.pallas import tpu as pltpu
from jax.sharding import PartitionSpec as P

EPSILON = 1e-06
BASIS_WIDTH = 0.6
BASIS_REACH = 6.0
F32 = jnp.float32
BF16 = jnp.bfloat16
MESH = pl.DeviceIdType.MESH


def dot(left, right):
    return jnp.dot(left, right, preferred_element_type=F32)


def dot_nt(left, right):
    return lax.dot_general(left, right, (((1,), (1,)), ((), ())), preferred_element_type=F32)


def dot_tn(left, right):
    return lax.dot_general(left, right, (((0,), (0,)), ((), ())), preferred_element_type=F32)


def gate(values):
    return 0.5 * jnp.tanh(0.5 * values) + 0.5


def split_two(values):
    high = values.astype(BF16)
    low = (values - high.astype(F32)).astype(BF16)
    return high, low


def onehot(mask):
    return jnp.where(mask, 1.0, 0.0).astype(BF16)


def body(
    n_space, n_image,
    pos_hbm, vel_hbm, emb_hbm, nb_hbm, up_hbm, down_hbm, climb_hbm, reset_hbm,
    fin_hbm, fout_hbm, uw_hbm, read_hbm, spring_hbm, step_hbm, mix_hbm,
    newpos_ref, newvel_ref, energy_ref,
    pos_ref, vel_ref, emb_ref, nb_t, up_ref, down_ref, climb_ref, reset_ref,
    fin_ref, fout_ref, uw_ref, read_ref, spring_ref, step_ref, mix_ref, fetch_sem,
    pos8, prev8, next8, coord, coord_src, ext_emb, emb_src, ext_hid, hid_src,
    grad_all, grad_src, grad_in, force_src, force_in,
    sel, sel_t, oh, oht, pv_all, slope_all, pre_two, ds_one, ds_two,
    rows_one, rows_two, filt_two, drad, w_in, w_back,
    norm_src, norm_in, sum_src, sum_in, band_src, band_in,
    send, recv, norm_send, norm_recv, sum_send, sum_recv, band_send, band_recv,
):
    domain = lax.axis_index("space")
    image = lax.axis_index("image")
    upper = lax.rem(domain + 1, n_space)
    lower = lax.rem(domain + n_space - 1, n_space)
    following = lax.rem(image + 1, n_image)
    previous = lax.rem(image + n_image - 1, n_image)
    per_atom, atoms = nb_t.shape
    ext = 3 * atoms
    chunks, pairs = oh.shape[0], oh.shape[1]
    basis = fin_ref.shape[1]
    channels = emb_ref.shape[1]

    sources = (
        pos_hbm, vel_hbm, emb_hbm, nb_hbm, up_hbm, down_hbm, climb_hbm, reset_hbm,
        fin_hbm, fout_hbm, uw_hbm, read_hbm, spring_hbm, step_hbm, mix_hbm,
    )
    targets = (
        pos_ref, vel_ref, emb_ref, nb_t, up_ref, down_ref, climb_ref, reset_ref,
        fin_ref, fout_ref, uw_ref, read_ref, spring_ref, step_ref, mix_ref,
    )
    fetches = [
        pltpu.make_async_copy(source, target, fetch_sem.at[i])
        for i, (source, target) in enumerate(zip(sources, targets))
    ]
    for i in (0, 4, 5, 2, 3, 8, 9, 10, 1, 11, 6, 7, 12, 13, 14):
        fetches[i].start()

    barrier = pltpu.get_barrier_semaphore()
    for i in range(1, n_space):
        pl.semaphore_signal(
            barrier, inc=1, device_id={"space": lax.rem(domain + i, n_space)}, device_id_type=MESH
        )
    for i in range(1, n_image):
        pl.semaphore_signal(
            barrier, inc=1, device_id={"image": lax.rem(image + i, n_image)}, device_id_type=MESH
        )

    def remote(src, dst, slot, where):
        return pltpu.make_async_remote_copy(
            src_ref=src, dst_ref=dst, send_sem=send.at[slot], recv_sem=recv.at[slot],
            device_id=where, device_id_type=MESH,
        )

    def spread(src, dst, out_sem, in_sem, axis, me, count):
        copies = []
        for i in range(1, count):
            copies.append(
                pltpu.make_async_remote_copy(
                    src_ref=src, dst_ref=dst.at[me], send_sem=out_sem.at[i], recv_sem=in_sem.at[me],
                    device_id={axis: lax.rem(me + i, count)}, device_id_type=MESH,
                )
            )
        for copy in copies:
            copy.start()
        dst[me] = src[...]

        def finish():
            for i in range(1, count):
                other = lax.rem(me + i, count)
                pltpu.make_async_remote_copy(
                    src_ref=src, dst_ref=dst.at[other], send_sem=out_sem.at[i],
                    recv_sem=in_sem.at[other], device_id={axis: other}, device_id_type=MESH,
                ).wait_recv()
            for copy in copies:
                copy.wait_send()

        return finish

    for i in (0, 4, 5, 2):
        fetches[i].wait()
    pos8[...] = jnp.zeros_like(pos8)
    for r in range(3):
        pos8[r : r + 1, :] = pos_ref[r]
    here = pos8[...]
    part_a = here.astype(BF16).astype(F32)
    rest = here - part_a
    part_b = rest.astype(BF16).astype(F32)
    part_c = rest - part_b
    parts = jnp.concatenate([part_a, part_b, part_c, jnp.zeros_like(here)], axis=0).astype(BF16)
    coord[0] = parts
    atom_rows = lax.broadcasted_iota(jnp.int32, (atoms, atoms), 0)
    embed = emb_ref[...]
    ext_emb[0:atoms, :] = embed
    for side, ids in ((0, up_ref), (1, down_ref)):
        picked = jnp.where(atom_rows == ids[...], 1.0, 0.0)
        sel_t[side] = picked.astype(BF16)
        sel[side] = picked.T.astype(BF16)
        coord_src[side] = dot(parts, sel_t[side]).astype(BF16)
        emb_src[side] = dot(sel[side], embed).astype(BF16)

    pl.semaphore_wait(barrier, n_space + n_image - 2)
    to_up, to_down = {"space": upper}, {"space": lower}
    coord_copies = [
        remote(coord_src.at[0], coord.at[1], 0, to_up),
        remote(coord_src.at[1], coord.at[2], 1, to_down),
    ]
    emb_copies = [
        remote(emb_src.at[0], ext_emb.at[pl.ds(atoms, atoms)], 2, to_up),
        remote(emb_src.at[1], ext_emb.at[pl.ds(2 * atoms, atoms)], 3, to_down),
    ]
    image_copies = [
        remote(pos8, prev8, 4, {"image": following}),
        remote(pos8, next8, 5, {"image": previous}),
    ]
    for copy in coord_copies + emb_copies + image_copies:
        copy.start()

    for i in (3, 8, 9, 10, 1, 11, 6, 7, 12, 13, 14):
        fetches[i].wait()
    nb = nb_t[...].T
    per_chunk = pairs // atoms
    ext_lane = lax.broadcasted_iota(jnp.int32, (atoms, ext), 1)
    for k in range(per_atom):
        c, r = k // per_chunk, k % per_chunk
        oh[c, r * atoms : (r + 1) * atoms, :] = onehot(nb[:, k : k + 1] == ext_lane)
    ext_row = lax.broadcasted_iota(jnp.int32, (ext, pairs), 0)
    def slot_row(c):
        return jnp.concatenate(
            [nb_t[pl.ds(c * per_chunk + r, 1), :] for r in range(per_chunk)], axis=1
        )

    def build(c, carry):
        oht[c] = onehot(slot_row(c) == ext_row)
        return carry

    lax.fori_loop(0, chunks, build, 0, unroll=1)
    for layer in range(2):
        high, low = split_two(fin_ref[layer])
        lanes = slice(layer * channels, (layer + 1) * channels)
        w_in[:, lanes] = jnp.concatenate([high, high, low], axis=0)
        w_back[layer] = jnp.concatenate([high, low], axis=0)

    for copy in coord_copies + emb_copies:
        copy.wait_recv()

    low_shift = jnp.where(domain == 0, -n_space, 0).astype(F32)
    high_shift = jnp.where(domain == n_space - 1, n_space, 0).astype(F32)
    all_coord = jnp.concatenate([coord[0], coord[1], coord[2]], axis=1)
    here_wide = jnp.concatenate([here] * per_chunk, axis=1)
    first_row = lax.broadcasted_iota(jnp.int32, (8, pairs), 0) == 0
    centres = lax.broadcasted_iota(jnp.int32, (basis, pairs), 0).astype(F32) * (
        BASIS_REACH / (basis - 1)
    )
    ext_embed = ext_emb[...]
    fout_one, fout_two = fout_ref[0], fout_ref[1]

    def fold(values):
        total = values[0:atoms]
        for r in range(1, per_chunk):
            total = total + values[r * atoms : (r + 1) * atoms]
        return total

    def repeat(values):
        return jnp.concatenate([values] * per_chunk, axis=0)

    def layer_one(c, total):
        found = dot(all_coord, oht[c])
        slots = slot_row(c)
        shift = jnp.where(
            slots >= 2 * atoms, high_shift, jnp.where(slots >= atoms, low_shift, 0.0)
        )
        there = found[0:8] + found[8:16] + found[16:24]
        vec = there + jnp.where(first_row, shift, 0.0) - here_wide
        pv_all[c] = vec
        sq_dist = jnp.sum(vec * vec, axis=0, keepdims=True)
        scaled = (sq_dist - centres) * (1.0 / BASIS_WIDTH)
        radial = jnp.exp(-scaled * scaled)
        slope_all[c] = radial * (-2.0 / BASIS_WIDTH) * scaled
        high, low = split_two(radial)
        pre = dot_tn(jnp.concatenate([high, low, high], axis=0), w_in[...])
        pre_two[c] = pre[:, channels:]
        pre_one = pre[:, :channels]
        sig = gate(pre_one)
        act = pre_one * sig
        sig, act = sig.astype(BF16), act.astype(BF16)
        ds_one[c] = sig + act * (1.0 - sig)
        filt = dot(act, fout_one)
        rows = dot(oh[c], ext_embed)
        rows_one[c] = rows.astype(BF16)
        return total + fold(filt * rows)

    zeros = jnp.zeros((atoms, channels), F32)
    msg_one = lax.fori_loop(0, chunks, layer_one, zeros, unroll=2)
    upd_one = dot(msg_one.astype(BF16), uw_ref[0])
    sig_one = gate(upd_one)
    act_one = upd_one * sig_one
    slope_one = sig_one + act_one * (1.0 - sig_one)
    hidden = (embed.astype(F32) + act_one).astype(BF16)
    ext_hid[0:atoms, :] = hidden
    hid_src[0] = dot(sel[0], hidden).astype(BF16)
    hid_src[1] = dot(sel[1], hidden).astype(BF16)
    hid_copies = [
        remote(hid_src.at[0], ext_hid.at[pl.ds(atoms, atoms)], 6, to_up),
        remote(hid_src.at[1], ext_hid.at[pl.ds(2 * atoms, atoms)], 7, to_down),
    ]
    for copy in hid_copies:
        copy.start()

    for copy in image_copies:
        copy.wait_recv()
    ahead = jnp.where(image == n_image - 1, 0.0, next8[...]) - here
    behind = here - jnp.where(image == 0, 0.0, prev8[...])
    row8 = lax.broadcasted_iota(jnp.int32, (8, atoms), 0)

    def place(values):
        block = jnp.zeros((8, atoms), F32)
        for r, value in enumerate(values):
            block = jnp.where(row8 == r, value, block)
        return block

    def rows_sum(values):
        return jnp.sum(values, axis=0, keepdims=True)

    norm_src[...] = place([rows_sum(ahead * ahead), rows_sum(behind * behind)])
    norm_done = spread(norm_src, norm_in, norm_send, norm_recv, "space", domain, n_space)

    def filter_two(c, carry):
        pre = pre_two[c]
        sig = gate(pre)
        act = pre * sig
        sig, act = sig.astype(BF16), act.astype(BF16)
        ds_two[c] = sig + act * (1.0 - sig)
        filt_two[c] = dot(act, fout_two)
        return carry

    lax.fori_loop(0, chunks, filter_two, 0, unroll=2)
    for copy in hid_copies:
        copy.wait_recv()
    ext_hidden = ext_hid[...]

    def layer_two(c, total):
        rows = dot(oh[c], ext_hidden)
        rows_two[c] = rows.astype(BF16)
        return total + fold(filt_two[c] * rows)

    msg_two = lax.fori_loop(0, chunks, layer_two, zeros, unroll=2)
    upd_two = dot(msg_two.astype(BF16), uw_ref[1])
    sig_two = gate(upd_two)
    act_two = upd_two * sig_two
    readout = read_ref[...]
    energy_row = rows_sum(act_two * readout)
    dupd_two = ((sig_two + act_two * (1.0 - sig_two)) * readout).astype(BF16)
    dmsg_two = dot_nt(dupd_two, uw_ref[1])

    grad_all[...] = jnp.zeros_like(grad_all)
    group = 2

    def scatter_two(g, carry):
        picks, sources = [], []
        for i in range(group):
            c = g * group + i
            picks.append(oht[c])
            sources.append((filt_two[c] * repeat(dmsg_two)).astype(BF16))
        grad_all[...] += dot(
            jnp.concatenate(picks, axis=1), jnp.concatenate(sources, axis=0)
        )
        return carry

    lax.fori_loop(0, chunks // group, scatter_two, 0)
    grad_src[0] = grad_all[atoms : 2 * atoms, :].astype(BF16)
    grad_src[1] = grad_all[2 * atoms : 3 * atoms, :].astype(BF16)
    grad_copies = [
        remote(grad_src.at[0], grad_in.at[0], 8, to_down),
        remote(grad_src.at[1], grad_in.at[1], 9, to_up),
    ]
    for copy in grad_copies:
        copy.start()

    def back(dmsg, rows, weight, slope, layer):
        dact = dot_nt(repeat(dmsg) * rows, weight)
        dpre = dact.astype(BF16) * slope
        both = dot_nt(w_back[layer], dpre)
        return both[:basis] + both[basis:]

    def back_two(c, carry):
        drad[c] = back(dmsg_two_low, rows_two[c], fout_two, ds_two[c], 1)
        return carry

    dmsg_two_low = dmsg_two.astype(BF16)
    lax.fori_loop(0, chunks, back_two, 0, unroll=2)
    for copy in grad_copies:
        copy.wait_recv()
    dhidden = grad_all[0:atoms, :] + dot(sel_t[0], grad_in[0]) + dot(sel_t[1], grad_in[1])
    dupd_one = (dhidden * slope_one).astype(BF16)
    dmsg_one = dot_nt(dupd_one, uw_ref[0]).astype(BF16)

    def back_one(c, carry):
        own, scattered = carry
        dradial = drad[c] + back(dmsg_one, rows_one[c], fout_one, ds_one[c], 0)
        dsq = jnp.sum(dradial * slope_all[c], axis=0, keepdims=True)
        pair = (2.0 * dsq) * pv_all[c]
        for r in range(per_chunk):
            own = own + pair[:, r * atoms : (r + 1) * atoms]
        high = pair.astype(BF16).astype(F32)
        both = jnp.concatenate([high, pair - high], axis=0).astype(BF16)
        return own, scattered + dot(both, oh[c])

    own, scattered = lax.fori_loop(
        0, chunks, back_one, (jnp.zeros((8, atoms), F32), jnp.zeros((16, ext), F32)),
        unroll=2,
    )
    scattered = scattered[0:8] + scattered[8:16]
    force_src[0] = scattered[:, atoms : 2 * atoms]
    force_src[1] = scattered[:, 2 * atoms : 3 * atoms]
    force_copies = [
        remote(force_src.at[0], force_in.at[0], 10, to_down),
        remote(force_src.at[1], force_in.at[1], 11, to_up),
    ]
    for copy in force_copies:
        copy.start()

    norm_done()
    norm_sum = norm_in[0]
    for i in range(1, n_space):
        norm_sum = norm_sum + norm_in[i]
    norms = jnp.sqrt(jnp.sum(norm_sum, axis=1, keepdims=True) + EPSILON)
    ahead_norm, behind_norm = norms[0:1], norms[1:2]
    tangent = ahead / ahead_norm + behind / behind_norm
    tangent_row = rows_sum(tangent * tangent)
    speed = place([vel_ref[r] for r in range(3)])
    speed_row = rows_sum(speed * speed)
    spring_part = spring_ref[...] * (ahead_norm - behind_norm)
    local_force = own - scattered[:, 0:atoms]
    for copy in force_copies:
        copy.wait_recv()

    def returned(side):
        ghost = force_in[side]
        high = ghost.astype(BF16).astype(F32)
        both = dot(jnp.concatenate([high, ghost - high], axis=0).astype(BF16), sel[side])
        return both[0:8] + both[8:16]

    forces = local_force - returned(0) - returned(1)
    sum_src[...] = place(
        [
            rows_sum(forces * forces), rows_sum(forces * tangent), tangent_row, energy_row,
            speed_row,
        ]
    )
    sum_done = spread(sum_src, sum_in, sum_send, sum_recv, "space", domain, n_space)
    sum_done()
    sums = sum_in[0]
    for i in range(1, n_space):
        sums = sums + sum_in[i]
    sums = jnp.sum(sums, axis=1, keepdims=True)
    force_sq, along, tangent_sq = sums[0:1], sums[1:2], sums[2:3]
    energy_ref[...] = sums[3:4]
    scale = 1.0 / jnp.sqrt(tangent_sq + EPSILON)
    parallel = along * scale
    unit_sq = tangent_sq * scale * scale
    climbing = climb_ref[...] > 0
    take = jnp.where(climbing, 2.0 * parallel, parallel - spring_part)
    movable = jnp.where((image > 0) & (image < n_image - 1), 1.0, 0.0)
    band_sq = jnp.maximum(force_sq - 2.0 * take * parallel + take * take * unit_sq, 0.0)
    band_src[...] = place([band_sq * movable, sums[4:5] * movable])
    band_done = spread(band_src, band_in, band_send, band_recv, "image", image, n_image)
    band_force = (forces - take * (tangent * scale)) * movable
    band_done()
    totals = band_in[0]
    for i in range(1, n_image):
        totals = totals + band_in[i]
    totals = jnp.sqrt(totals + EPSILON)
    force_norm, speed_norm = totals[0:1], totals[1:2]
    mixing = mix_ref[...]
    time_step = step_ref[...]
    mixed = (1.0 - mixing) * speed + mixing * (speed_norm / force_norm) * band_force
    kept = jnp.where(reset_ref[...] > 0, 0.0, mixed)
    new_speed = (kept + time_step * band_force) * movable
    new_place = here + time_step * new_speed
    for r in range(3):
        newvel_ref[r] = new_speed[r : r + 1]
        newpos_ref[r] = new_place[r : r + 1]
    for copy in (
        coord_copies + emb_copies + image_copies + hid_copies + grad_copies + force_copies
    ):
        copy.wait_send()


def per_device(
    n_space, n_image,
    positions, velocity, embed, neighbours, send_up, send_down, climb, reset,
    filter_in, filter_out, update_weight, readout, spring, time_step, mixing,
):
    atoms, per_atom = neighbours.shape
    channels = embed.shape[1]
    basis = filter_in.shape[1]
    per_chunk = 16
    chunks, pairs = per_atom // per_chunk, per_chunk * atoms
    ext = 3 * atoms
    vmem = pl.BlockSpec(memory_space=pltpu.VMEM)
    hbm = pl.BlockSpec(memory_space=pltpu.HBM)
    dma = pltpu.SemaphoreType.DMA
    basis_shape = filter_in.shape
    scratch = [
        pltpu.VMEM((3, 1, atoms), F32),
        pltpu.VMEM((3, 1, atoms), F32),
        pltpu.VMEM((atoms, channels), BF16),
        pltpu.VMEM((per_atom, atoms), jnp.int32),
        pltpu.VMEM((1, atoms), jnp.int32),
        pltpu.VMEM((1, atoms), jnp.int32),
        pltpu.VMEM((1, 1), jnp.int32),
        pltpu.VMEM((1, 1), jnp.int32),
        pltpu.VMEM(basis_shape, F32),
        pltpu.VMEM((2, channels, channels), BF16),
        pltpu.VMEM((2, channels, channels), BF16),
        pltpu.VMEM((1, channels), F32),
        pltpu.VMEM((1, 1), F32),
        pltpu.VMEM((1, 1), F32),
        pltpu.VMEM((1, 1), F32),
        dma((15,)),
        pltpu.VMEM((8, atoms), F32),
        pltpu.VMEM((8, atoms), F32),
        pltpu.VMEM((8, atoms), F32),
        pltpu.VMEM((3, 32, atoms), BF16),
        pltpu.VMEM((2, 32, atoms), BF16),
        pltpu.VMEM((ext, channels), BF16),
        pltpu.VMEM((2, atoms, channels), BF16),
        pltpu.VMEM((ext, channels), BF16),
        pltpu.VMEM((2, atoms, channels), BF16),
        pltpu.VMEM((ext, channels), F32),
        pltpu.VMEM((2, atoms, channels), BF16),
        pltpu.VMEM((2, atoms, channels), BF16),
        pltpu.VMEM((2, 8, atoms), F32),
        pltpu.VMEM((2, 8, atoms), F32),
        pltpu.VMEM((2, atoms, atoms), BF16),
        pltpu.VMEM((2, atoms, atoms), BF16),
        pltpu.VMEM((chunks, pairs, ext), BF16),
        pltpu.VMEM((chunks, ext, pairs), BF16),
        pltpu.VMEM((chunks, 8, pairs), F32),
        pltpu.VMEM((chunks, basis, pairs), F32),
        pltpu.VMEM((chunks, pairs, channels), F32),
        pltpu.VMEM((chunks, pairs, channels), BF16),
        pltpu.VMEM((chunks, pairs, channels), BF16),
        pltpu.VMEM((chunks, pairs, channels), BF16),
        pltpu.VMEM((chunks, pairs, channels), BF16),
        pltpu.VMEM((chunks, pairs, channels), F32),
        pltpu.VMEM((chunks, basis, pairs), F32),
        pltpu.VMEM((3 * basis, 2 * channels), BF16),
        pltpu.VMEM((2, 2 * basis, channels), BF16),
        pltpu.VMEM((8, atoms), F32),
        pltpu.VMEM((n_space, 8, atoms), F32),
        pltpu.VMEM((8, atoms), F32),
        pltpu.VMEM((n_space, 8, atoms), F32),
        pltpu.VMEM((8, atoms), F32),
        pltpu.VMEM((n_image, 8, atoms), F32),
        dma((12,)), dma((12,)),
        dma((n_space,)), dma((n_space,)),
        dma((n_space,)), dma((n_space,)),
        dma((n_image,)), dma((n_image,)),
    ]
    new_pos, new_vel, energy = pl.pallas_call(
        functools.partial(body, n_space, n_image),
        out_shape=(
            jax.ShapeDtypeStruct((3, 1, atoms), F32),
            jax.ShapeDtypeStruct((3, 1, atoms), F32),
            jax.ShapeDtypeStruct((1, 1), F32),
        ),
        in_specs=[hbm] * 15,
        out_specs=(vmem, vmem, vmem),
        scratch_shapes=scratch,
        compiler_params=pltpu.CompilerParams(
            collective_id=0, has_side_effects=True, vmem_limit_bytes=60 * 1024 * 1024
        ),
    )(
        jnp.transpose(positions, (1, 0, 2)), jnp.transpose(velocity, (1, 0, 2)), embed,
        neighbours.T, send_up.reshape(1, -1), send_down.reshape(1, -1), climb.reshape(1, 1), reset.reshape(1, 1),
        filter_in, filter_out, update_weight, readout.reshape(1, -1),
        spring.reshape(1, 1), time_step.reshape(1, 1), mixing.reshape(1, 1),
    )
    back = (1, 0, 2)
    return jnp.transpose(new_pos, back), jnp.transpose(new_vel, back), energy.reshape(1)


def solution(mesh):
    placed = (
        P("image", None, "space"), P("image", None, "space"), P("space", None), P("space", None),
        P("space"), P("space"), P("image"), P("image"), P(), P(), P(), P(), P(), P(), P(),
    )
    return jax.shard_map(
        functools.partial(per_device, mesh.shape["space"], mesh.shape["image"]),
        mesh=mesh,
        in_specs=placed,
        out_specs=(P("image", None, "space"), P("image", None, "space"), P("image")),
        check_vma=False,
    )
```
